32 devices in a mesh: group: 2 (over y), tile: 8 (over z, x), strip: 2 (over core).
Axes of the slice: x: 2, y: 2, z: 4, core: 2. Of those that a mesh axis runs over, the one named last changes fastest.
Arguments:
- image: bfloat16 [128, 256, 256], P(('group', 'strip'), 'tile'), parts along dimension 0, may hold values from -16 to 16
- bn_gain: float32 [256], replicated, may hold values from 0.25 to 1.75
- bn_shift: float32 [256], replicated, may hold values from -3 to 3
- w_expand: bfloat16 [256, 1024], replicated, may hold values from -0.375 to 0.375
- b_expand: float32 [1024], replicated, may hold values from -3 to 3
- w_depth: float32 [9, 1024], replicated, may hold values from -2 to 2
- b_depth: float32 [1024], replicated, may hold values from -3 to 3
- w_project: bfloat16 [1024, 256], replicated, may hold values from -0.1875 to 0.1875
- b_project: float32 [256], replicated, may hold values from -3 to 3
- attn_gain: float32 [256], replicated, may hold values from 0.25 to 1.75
- attn_shift: float32 [256], replicated, may hold values from -2 to 2
- w_qkv: bfloat16 [256, 768], replicated, may hold values from -0.375 to 0.375
- w_out: bfloat16 [256, 256], replicated, may hold values from -0.375 to 0.375
- rel_table: float32 [8, 225], replicated, may hold values from -4 to 304
- ffn_gain: float32 [256], replicated, may hold values from 0.25 to 1.75
- ffn_shift: float32 [256], replicated, may hold values from -2 to 2
- w_up: bfloat16 [256, 1024], replicated, may hold values from -0.375 to 0.375
- b_up: float32 [1024], replicated, may hold values from -3 to 3
- w_down: bfloat16 [1024, 256], replicated, may hold values from -0.1875 to 0.1875
- b_down: float32 [256], replicated, may hold values from -3 to 3
Outputs:
- block_out: bfloat16 [128, 256, 256], P(('group', 'strip'), 'tile'), parts along dimension 0
The draws below stay inside these ranges and needn't reach their ends.
There are 2 independent parts, one for each index of `group`. The reference program is written for one: setup_inputs(seed, part) draws one part's arguments, and reference() takes and returns one part's arrays. A program takes and returns all parts, laid end to end along the dimension named above; an argument that names none is the same for every part. Nothing has to cross between parts.
All inputs are finite; a program needn't handle non-finite values.
Results may differ from the reference program's by a relative error of at most 0.0064.
Values may be sent and summed in bfloat16 or wider, within the bound.
No kernel may reach another device: no remote copies, remote signals or barrier semaphores. Data moves between devices by JAX's collectives and lax.ppermute only.
A program may use at most 64 MiB of HBM per device.

```python
import math
import jax
import jax.numpy as jnp
from jax import lax

C = 256
E = 1024
F = 1024
GRID = 8
TW = 32
HEADS = 8
H = 64
W = 256


def draw_image(key, part):
    key_noise = jax.random.fold_in(key, 11)
    key_token = jax.random.fold_in(key, 12)
    key_channel = jax.random.fold_in(key, 13)
    low_log = math.log(0.3)
    high_log = math.log(3.0)
    chan_scale = jnp.exp(jax.random.uniform(key_channel, (C,), jnp.float32, low_log, high_log))
    token_scale = jnp.exp(jax.random.uniform(key_token, (H, W, 1), jnp.float32, low_log, high_log))
    noise = jax.random.normal(key_noise, (H, W, C), jnp.float32)
    pixels = noise * token_scale * chan_scale
    return jnp.clip(pixels, -16.0, 16.0).astype(jnp.bfloat16)


def draw_rel_table(key, part):
    entries = (2 * GRID - 1) ** 2
    key_base = jax.random.fold_in(key, 21)
    base_table = jnp.clip(jax.random.normal(key_base, (HEADS, entries), jnp.float32), -4.0, 4.0)
    return base_table.astype(jnp.float32)


def gaussian(own_key, dims, scale, limit, held_as=jnp.bfloat16):
    return jnp.clip(scale * jax.random.normal(own_key, dims, jnp.float32), -limit, limit).astype(held_as)


def setup_inputs(seed: int = 0, part: int = 0) -> dict:
    keys = jax.random.split(jax.random.key(seed), 21)
    part_keys = jax.random.split(jax.random.fold_in(keys[20], part), 21)
    return {
        "image": draw_image(jax.random.fold_in(jax.random.fold_in(keys[20], part), 71), part),
        "bn_gain": jnp.clip(1.0 + 0.15 * jax.random.normal(keys[1], (C,), jnp.float32), 0.25, 1.75),
        "bn_shift": gaussian(keys[2], (C,), 0.5, 3.0, jnp.float32),
        "w_expand": gaussian(keys[3], (C, E), C ** -0.5, 0.375),
        "b_expand": gaussian(keys[4], (E,), 0.5, 3.0, jnp.float32),
        "w_depth": gaussian(keys[5], (9, E), 9 ** -0.5, 2.0, jnp.float32),
        "b_depth": gaussian(keys[6], (E,), 0.5, 3.0, jnp.float32),
        "w_project": gaussian(keys[7], (E, C), E ** -0.5, 0.1875),
        "b_project": gaussian(keys[8], (C,), 0.5, 3.0, jnp.float32),
        "attn_gain": jnp.clip(1.0 + 0.15 * jax.random.normal(keys[9], (C,), jnp.float32), 0.25, 1.75),
        "attn_shift": gaussian(keys[10], (C,), 0.3, 2.0, jnp.float32),
        "w_qkv": gaussian(keys[11], (C, 3 * C), C ** -0.5, 0.375),
        "w_out": gaussian(keys[12], (C, C), C ** -0.5, 0.375),
        "rel_table": draw_rel_table(jax.random.fold_in(keys[20], 71), part),
        "ffn_gain": jnp.clip(1.0 + 0.15 * jax.random.normal(keys[14], (C,), jnp.float32), 0.25, 1.75),
        "ffn_shift": gaussian(keys[15], (C,), 0.3, 2.0, jnp.float32),
        "w_up": gaussian(keys[16], (C, F), C ** -0.5, 0.375),
        "b_up": gaussian(keys[17], (F,), 0.5, 3.0, jnp.float32),
        "w_down": gaussian(keys[18], (F, C), F ** -0.5, 0.1875),
        "b_down": gaussian(keys[19], (C,), 0.5, 3.0, jnp.float32),
    }


EPSILON = 1e-05

def gelu_tanh(inputs):
    return jax.nn.gelu(inputs, approximate=True)

def layer_norm(inputs, norm_gain, norm_shift):
    center = lax.optimization_barrier(jnp.mean(inputs, axis=-1, keepdims=True))
    spread = lax.optimization_barrier(jnp.mean(jnp.square(inputs - center), axis=-1, keepdims=True))
    return (inputs - center) * lax.rsqrt(spread + EPSILON) * norm_gain + norm_shift

def expand_tokens(pixels, bn_gain, bn_shift, w_expand, b_expand):
    normed = (pixels.astype(jnp.float32) * bn_gain + bn_shift).astype(jnp.bfloat16)
    pre_act = jnp.dot(normed, w_expand, preferred_element_type=jnp.float32) + b_expand
    return gelu_tanh(pre_act).astype(jnp.bfloat16)

def depthwise(framed, w_depth, b_depth):
    out_rows = framed.shape[0] - 2
    out_cols = framed.shape[1] - 2
    accum_sum = jnp.zeros((out_rows, out_cols, framed.shape[2]), jnp.float32) + b_depth
    for row_step in range(3):
        for col_step in range(3):
            window_part = framed[row_step:row_step + out_rows, col_step:col_step + out_cols]
            accum_sum = accum_sum + window_part.astype(jnp.float32) * w_depth[row_step * 3 + col_step]
    return gelu_tanh(accum_sum).astype(jnp.bfloat16)

def position_bias(rel_table):
    grid_side = GRID
    token_ids = jnp.arange(grid_side * grid_side, dtype=jnp.int32)
    row_of = token_ids // grid_side
    col_of = token_ids % grid_side
    offset = (row_of[:, None] - row_of[None, :] + grid_side - 1) * (2 * grid_side - 1) + (col_of[:, None] - col_of[None, :] + grid_side - 1)
    entry_ids = jnp.arange((2 * grid_side - 1) ** 2, dtype=jnp.int32)
    onehot = (offset.reshape(-1)[:, None] == entry_ids[None, :]).astype(jnp.float32)
    pos_bias = jnp.dot(rel_table, onehot.T, precision=lax.Precision.HIGHEST, preferred_element_type=jnp.float32)
    return pos_bias.reshape(rel_table.shape[0], grid_side * grid_side, grid_side * grid_side)

def grid_attention(windows, attn_gain, attn_shift, w_qkv, w_out, pos_bias):
    win_count = windows.shape[0]
    places = windows.shape[1]
    model_width = windows.shape[2]
    head_count = pos_bias.shape[0]
    head_size = model_width // head_count
    normed = layer_norm(windows.astype(jnp.float32), attn_gain, attn_shift).astype(jnp.bfloat16)
    projected_qkv = jnp.dot(normed, w_qkv, preferred_element_type=jnp.float32)
    queries = (projected_qkv[..., :model_width] * head_size ** (-0.5)).astype(jnp.bfloat16)
    key_heads = projected_qkv[..., model_width:2 * model_width].astype(jnp.bfloat16)
    value_heads = projected_qkv[..., 2 * model_width:].astype(jnp.bfloat16)
    queries = queries.reshape(win_count, places, head_count, head_size).astype(jnp.float32)
    key_heads = key_heads.reshape(win_count, places, head_count, head_size).astype(jnp.float32)
    value_heads = value_heads.reshape(win_count, places, head_count, head_size).astype(jnp.float32)
    scores = jnp.einsum('wihd,wjhd->whij', queries, key_heads, precision=lax.Precision.HIGHEST) + pos_bias[None]
    row_peak = lax.optimization_barrier(jnp.max(scores, axis=-1, keepdims=True))
    exp_scores = jnp.exp(scores - row_peak)
    weights_bf = (exp_scores / lax.optimization_barrier(jnp.sum(exp_scores, axis=-1, keepdims=True))).astype(jnp.bfloat16)
    context = jnp.einsum('whij,wjhd->wihd', weights_bf.astype(jnp.float32), value_heads, precision=lax.Precision.HIGHEST)
    context = context.astype(jnp.bfloat16).reshape(win_count, places, model_width)
    attended = windows.astype(jnp.float32) + jnp.dot(context, w_out, preferred_element_type=jnp.float32)
    return attended.astype(jnp.bfloat16)

def feed_forward(tokens_in, ffn_gain, ffn_shift, w_up, b_up, w_down, b_down):
    normed = layer_norm(tokens_in.astype(jnp.float32), ffn_gain, ffn_shift).astype(jnp.bfloat16)
    hidden = gelu_tanh(jnp.dot(normed, w_up, preferred_element_type=jnp.float32) + b_up).astype(jnp.bfloat16)
    result = tokens_in.astype(jnp.float32) + jnp.dot(hidden, w_down, preferred_element_type=jnp.float32) + b_down
    return result.astype(jnp.bfloat16)

def reference(image, bn_gain, bn_shift, w_expand, b_expand, w_depth, b_depth, w_project, b_project, attn_gain, attn_shift, w_qkv, w_out, rel_table, ffn_gain, ffn_shift, w_up, b_up, w_down, b_down):
    height = image.shape[0]
    width_all = image.shape[1]
    channels = image.shape[2]
    blocks = width_all // TW
    padded = jnp.pad(image, ((0, 0), (1, 1), (0, 0)))

    def column_block(block_at):
        start_col = (block_at * TW).astype(jnp.int32)
        window_cols = lax.dynamic_slice_in_dim(padded, start_col, TW + 2, 1)
        expanded = expand_tokens(window_cols, bn_gain, bn_shift, w_expand, b_expand)
        col_index = start_col - 1 + jnp.arange(TW + 2, dtype=jnp.int32)
        inside = (col_index >= 0) & (col_index < width_all)
        expanded = jnp.where(inside[None, :, None], expanded, jnp.zeros((), jnp.bfloat16))
        expanded = jnp.pad(expanded, ((1, 1), (0, 0), (0, 0)))
        hidden = depthwise(expanded, w_depth, b_depth)
        projected = jnp.dot(hidden, w_project, preferred_element_type=jnp.float32) + b_project
        return (window_cols[:, 1:-1].astype(jnp.float32) + projected).astype(jnp.bfloat16)
    section_one = lax.map(column_block, jnp.arange(blocks, dtype=jnp.int32))
    section_one = section_one.transpose(1, 0, 2, 3).reshape(height, width_all, channels)
    across = height // GRID
    along_cols = width_all // GRID
    windows = section_one.reshape(GRID, across, GRID, along_cols, channels).transpose(1, 3, 0, 2, 4)
    total_windows = across * along_cols
    windows = windows.reshape(total_windows, GRID * GRID, channels)
    pos_bias = position_bias(rel_table)
    per_block = math.gcd(total_windows, 64)
    grouped = windows.reshape(total_windows // per_block, per_block, GRID * GRID, channels)

    def window_block(window_group):
        attended = grid_attention(window_group, attn_gain, attn_shift, w_qkv, w_out, pos_bias)
        return feed_forward(attended, ffn_gain, ffn_shift, w_up, b_up, w_down, b_down)
    result = lax.map(window_block, grouped)
    result = result.reshape(across, along_cols, GRID, GRID, channels).transpose(2, 0, 3, 1, 4)
    return result.reshape(height, width_all, channels)
```

```python
import functools

import jax
import jax.numpy as jnp
from jax import lax
from jax.experimental import pallas as pl
from jax.experimental.pallas import tpu as pltpu
from jax.sharding import PartitionSpec as P

GRID = 8
EPSILON = 1e-05
F32 = jnp.float32
BF16 = jnp.bfloat16
SLAB = 8
LANES = 128
VMEM_LIMIT = 48 * 1024 * 1024


def dot(lhs, rhs):
    return jnp.dot(lhs, rhs, preferred_element_type=F32)


def dot_nt(lhs, rhs):
    return lax.dot_general(lhs, rhs, (((1,), (1,)), ((), ())), preferred_element_type=F32)


def gelu(v):
    half = 0.5 * v
    inner = v * (0.7978845608028654 + (0.7978845608028654 * 0.044715) * (v * v))
    return half + half * jnp.tanh(inner)


def layer_norm(x, gain, shift):
    center = jnp.mean(x, axis=-1, keepdims=True)
    diff = x - center
    spread = jnp.mean(diff * diff, axis=-1, keepdims=True)
    return diff * lax.rsqrt(spread + EPSILON) * gain + shift


def full(shape):
    return pl.BlockSpec(shape, lambda *_: (0,) * len(shape))


SMEM = pl.BlockSpec(memory_space=pltpu.SMEM)
PARAMS = pltpu.CompilerParams(vmem_limit_bytes=VMEM_LIMIT)


def edges_kernel(image_ref, up_ref, down_ref, out_ref):
    rows, cols, width = image_ref.shape
    pixels = image_ref[...].reshape(rows * cols, width)
    pick = lax.broadcasted_iota(jnp.int32, (2 * rows, rows * cols), 0)
    place = lax.broadcasted_iota(jnp.int32, (2 * rows, rows * cols), 1)
    wanted = jnp.where(pick < rows, pick * cols, (pick - rows) * cols + cols - 1)
    onehot = jnp.where(place == wanted, 1.0, 0.0).astype(BF16)
    columns = dot(onehot, pixels)
    up = up_ref[...].astype(F32)
    down = down_ref[...].astype(F32)
    for side, col in ((0, 0), (1, cols - 1)):
        corner_up = jnp.broadcast_to(up[col : col + 1], (SLAB, width))
        corner_down = jnp.broadcast_to(down[col : col + 1], (SLAB, width))
        out_ref[side] = jnp.concatenate(
            [columns[side * rows : (side + 1) * rows], corner_up, corner_down], axis=0
        ).astype(BF16)


def edges(image, up, down):
    rows, cols, width = image.shape
    return pl.pallas_call(
        edges_kernel,
        out_shape=jax.ShapeDtypeStruct((2, rows + 2 * SLAB, width), BF16),
        compiler_params=PARAMS,
        name="edges",
    )(image, up, down)


def expand_block(pixels, gain, shift, w_ref, b_ref, store):
    normed = (pixels.astype(F32) * gain + shift).astype(BF16)
    step = 2 * LANES
    for n in range(w_ref.shape[1] // step):
        part = slice(n * step, (n + 1) * step)
        store(part, gelu(dot(normed, w_ref[:, part]) + b_ref[:, part]))


def expand_kernel(image_ref, gain_ref, shift_ref, w_ref, b_ref, out_ref):
    def store(part, value):
        out_ref[:, part] = value.astype(BF16)

    expand_block(image_ref[...], gain_ref[...], shift_ref[...], w_ref, b_ref, store)


def expand(tokens, gain, shift, w_expand, b_expand):
    count, width = tokens.shape
    hidden = w_expand.shape[1]
    block = count // 4
    return pl.pallas_call(
        expand_kernel,
        grid=(4,),
        in_specs=[
            pl.BlockSpec((block, width), lambda i: (i, 0)),
            full((1, width)),
            full((1, width)),
            full((width, hidden)),
            full((1, hidden)),
        ],
        out_specs=pl.BlockSpec((block, hidden), lambda i: (i, 0)),
        out_shape=jax.ShapeDtypeStruct((count, hidden), BF16),
        compiler_params=PARAMS,
        cost_estimate=pl.CostEstimate(
            flops=2 * count * width * hidden, bytes_accessed=4_000_000, transcendentals=count * hidden
        ),
        name="expand",
    )(tokens, gain, shift, w_expand, b_expand)


def conv_kernel(
    piece,
    place_ref,
    expanded_ref,
    image_ref,
    left_ref,
    right_ref,
    up_ref,
    down_ref,
    gain_ref,
    shift_ref,
    w_expand_ref,
    b_expand_ref,
    w_depth_ref,
    b_depth_ref,
    w_project_ref,
    b_project_ref,
    out0_ref,
    out1_ref,
    out2_ref,
    out3_ref,
    rim_ref,
    side_ref,
    beyond_ref,
    tap_ref,
    deep_ref,
):
    rows, cols, width = image_ref.shape
    hidden = expanded_ref.shape[-1]
    places = 4
    groups = rows // SLAB
    first = piece * places
    zi, xc = place_ref[0], place_ref[1]
    ok_left, ok_right, ok_up, ok_down = (place_ref[2], place_ref[3], place_ref[4], place_ref[5])

    outer_ref = up_ref if piece == 0 else down_ref
    rim_in = jnp.concatenate([left_ref[...], right_ref[...], outer_ref[...]], axis=0)

    def store(part, value):
        rim_ref[:, part] = value.astype(BF16).astype(F32)

    expand_block(rim_in, gain_ref[...], shift_ref[...], w_expand_ref, b_expand_ref, store)
    ok_outer = ok_up if piece == 0 else ok_down
    tall = rows + 2 * SLAB
    beyond_ref[...] = jnp.where(ok_outer > 0, rim_ref[2 * tall : 2 * tall + cols, :], 0.0).astype(BF16)
    for side, ok in ((0, ok_left), (1, ok_right)):
        base = side * tall
        side_ref[1 : rows + 1, :] = jnp.where(ok > 0, rim_ref[base : base + rows, :], 0.0)
        side_ref[0:1, :] = jnp.where(ok * ok_up > 0, rim_ref[base + rows : base + rows + 1, :], 0.0)
        side_ref[rows + 1 : rows + 2, :] = jnp.where(
            ok * ok_down > 0, rim_ref[base + rows + SLAB : base + rows + SLAB + 1, :], 0.0
        )
        j = 2 * side
        tap_ref[side] = (
            side_ref[0:rows, :] * w_depth_ref[j : j + 1, :]
            + side_ref[1 : rows + 1, :] * w_depth_ref[3 + j : 4 + j, :]
            + side_ref[2 : rows + 2, :] * w_depth_ref[6 + j : 7 + j, :]
        )

    col_id = lax.broadcasted_iota(jnp.int32, (cols, LANES), 0)

    def chunk(index, carry):
        lanes = pl.ds(pl.multiple_of(index * LANES, LANES), LANES)
        weights = [w_depth_ref[t : t + 1, lanes] for t in range(9)]
        bias = b_depth_ref[:, lanes]
        for m in range(groups):
            above = m * SLAB + first - 1
            lines = []
            for q in range(places + 2):
                r = above + q
                if 0 <= r < rows:
                    lines.append(expanded_ref[r, :, lanes].astype(F32))
                else:
                    lines.append(beyond_ref[:, lanes].astype(F32))
            for q in range(places):
                r = above + 1 + q
                sums = [
                    lines[q] * weights[j] + lines[q + 1] * weights[3 + j] + lines[q + 2] * weights[6 + j]
                    for j in range(3)
                ]
                before = jnp.where(col_id == 0, tap_ref[0, r : r + 1, lanes], pltpu.roll(sums[0], 1, 0))
                after = jnp.where(
                    col_id == cols - 1, tap_ref[1, r : r + 1, lanes], pltpu.roll(sums[2], cols - 1, 0)
                )
                deep_ref[q, m, :, lanes] = gelu(before + sums[1] + after + bias).astype(BF16)
        return carry

    lax.fori_loop(0, hidden // LANES, chunk, 0)

    octets = cols // SLAB
    for k, out_ref in enumerate((out0_ref, out1_ref, out2_ref, out3_ref)):
        q = jnp.bitwise_xor(zi, k)
        projected = dot(deep_ref[q].reshape(groups * cols, hidden), w_project_ref[...]) + b_project_ref[...]
        own = jnp.stack([image_ref[m * SLAB + first + q] for m in range(groups)]).astype(F32)
        section = (own + projected.reshape(groups, cols, width)).reshape(groups, octets, SLAB, width)
        for o in range(octets):
            out_ref[jnp.bitwise_xor(xc, o)] = section[:, o].reshape(groups * SLAB, width).astype(BF16)


def conv(piece, place, expanded, image, left, right, up, down, weights):
    rows, cols, width = image.shape
    hidden = expanded.shape[-1]
    groups = rows // SLAB
    tall = rows + 2 * SLAB
    shape = jax.ShapeDtypeStruct((4, groups * SLAB, width), BF16)
    return pl.pallas_call(
        functools.partial(conv_kernel, piece),
        in_specs=[SMEM] + [pl.BlockSpec(memory_space=pltpu.VMEM)] * 14,
        out_specs=[pl.BlockSpec(memory_space=pltpu.VMEM)] * 4,
        out_shape=[shape] * 4,
        scratch_shapes=[
            pltpu.VMEM((2 * tall + cols, hidden), F32),
            pltpu.VMEM((rows + SLAB, hidden), F32),
            pltpu.VMEM((cols, hidden), BF16),
            pltpu.VMEM((2, rows, hidden), F32),
            pltpu.VMEM((4, groups, cols, hidden), BF16),
        ],
        compiler_params=PARAMS,
        cost_estimate=pl.CostEstimate(
            flops=rows * cols * width * hidden, bytes_accessed=6_000_000, transcendentals=rows * cols * hidden
        ),
        name="conv",
    )(place, expanded, image, left, right, up, down, *weights)


def attend_kernel(
    heads,
    place_ref,
    in0_ref,
    in1_ref,
    in2_ref,
    in3_ref,
    gain_ref,
    shift_ref,
    w_qkv_ref,
    w_out_ref,
    bias_ref,
    ffn_gain_ref,
    ffn_shift_ref,
    w_up_ref,
    b_up_ref,
    w_down_ref,
    b_down_ref,
    out0_ref,
    out1_ref,
    out2_ref,
    out3_ref,
    token_ref,
    normed_ref,
    query_t_ref,
    value_t_ref,
):
    zi, xc = place_ref[0], place_ref[1]
    halves, count, _ = normed_ref.shape
    width = halves * LANES
    chunk_rows = token_ref.shape[1]
    head = width // heads
    tokens = bias_ref.shape[1]
    wins = count // tokens

    for j, ref in enumerate((in0_ref, in1_ref, in2_ref, in3_ref)):
        for k in range(4):
            slot = jnp.bitwise_xor(zi, k) * 4 + jnp.bitwise_xor(xc, j)
            x = ref[k].astype(F32)
            token_ref[slot] = x
            normed = layer_norm(x, gain_ref[...], shift_ref[...])
            spot = pl.ds(pl.multiple_of(slot * chunk_rows, chunk_rows), chunk_rows)
            for c in range(halves):
                normed_ref[c, spot, :] = normed[:, c * LANES : (c + 1) * LANES]

    query_t_ref[...] = w_qkv_ref[:, :width].T
    value_t_ref[...] = w_qkv_ref[:, 2 * width :].T
    left_half = lax.broadcasted_iota(jnp.int32, (tokens, 2 * tokens), 1) < tokens
    row_head = lax.broadcasted_iota(jnp.int32, (LANES, 2 * tokens), 0) // head
    per_group = LANES // head

    for pair in range(wins // 2):
        spots = [pl.ds(2 * pair + w, tokens, stride=wins) for w in range(2)]
        columns = [jnp.concatenate([normed_ref[c, s, :] for s in spots], axis=0) for c in range(halves)]
        normed = jnp.concatenate(columns, axis=1).astype(BF16)
        keys = dot(normed, w_qkv_ref[:, width : 2 * width]).astype(BF16)
        query_t = (dot_nt(query_t_ref[...], normed) * head ** (-0.5)).astype(BF16)
        value_t = dot_nt(value_t_ref[...], normed).astype(BF16)
        parts = []
        for h in range(heads):
            g = h // per_group
            span = slice(g * LANES, (g + 1) * LANES)
            own = jnp.where(row_head == h % per_group, query_t[span], jnp.zeros((), BF16))
            both = dot(keys[:, span], own)
            scores = jnp.where(left_half, both[:tokens], both[tokens:]) + bias_ref[h]
            weight = jnp.exp(scores - jnp.max(scores, axis=0, keepdims=True))
            probs = weight * (1.0 / jnp.sum(weight, axis=0, keepdims=True))
            spread = jnp.concatenate(
                [jnp.where(left_half, probs, 0.0), jnp.where(left_half, 0.0, probs)], axis=0
            ).astype(BF16)
            parts.append(dot(value_t[h * head : (h + 1) * head], spread))
        context = jnp.concatenate(parts, axis=0).astype(BF16).T
        attended = dot(context, w_out_ref[...])
        for w, spot in enumerate(spots):
            for c in range(halves):
                normed_ref[c, spot, :] = attended[w * tokens : (w + 1) * tokens, c * LANES : (c + 1) * LANES]

    block = 4 * chunk_rows
    step = 2 * LANES
    for i in range(4):
        part = slice(i * block, (i + 1) * block)
        attended = jnp.concatenate([normed_ref[c, part, :] for c in range(halves)], axis=1)
        section = token_ref[4 * i : 4 * i + 4].reshape(block, width) + attended
        section = section.astype(BF16).astype(F32)
        normed = layer_norm(section, ffn_gain_ref[...], ffn_shift_ref[...]).astype(BF16)
        total = section + b_down_ref[...]
        for n in range(w_up_ref.shape[1] // step):
            inner = slice(n * step, (n + 1) * step)
            hidden = gelu(dot(normed, w_up_ref[:, inner]) + b_up_ref[:, inner]).astype(BF16)
            total = total + dot(hidden, w_down_ref[inner, :])
        token_ref[4 * i : 4 * i + 4] = total.reshape(4, chunk_rows, width)

    for j, ref in enumerate((out0_ref, out1_ref, out2_ref, out3_ref)):
        for k in range(4):
            slot = jnp.bitwise_xor(zi, k) * 4 + jnp.bitwise_xor(xc, j)
            ref[k] = token_ref[slot].astype(BF16)


def attend(place, arrived, heads, weights):
    chunk_rows, width = arrived[0].shape[1:]
    count = 16 * chunk_rows
    flops = 2 * count * width * (4 * width + 2 * weights[7].shape[1])
    shape = jax.ShapeDtypeStruct(arrived[0].shape, BF16)
    return pl.pallas_call(
        functools.partial(attend_kernel, heads),
        in_specs=[SMEM] + [pl.BlockSpec(memory_space=pltpu.VMEM)] * 15,
        out_specs=[pl.BlockSpec(memory_space=pltpu.VMEM)] * 4,
        out_shape=[shape] * 4,
        scratch_shapes=[
            pltpu.VMEM((16, chunk_rows, width), F32),
            pltpu.VMEM((width // LANES, count, LANES), F32),
            pltpu.VMEM((width, width), BF16),
            pltpu.VMEM((width, width), BF16),
        ],
        compiler_params=PARAMS,
        cost_estimate=pl.CostEstimate(flops=flops, bytes_accessed=4_000_000, transcendentals=count * 1024),
        name="attend",
    )(place, *arrived, *weights)


def gather_kernel(place_ref, *refs):
    out_ref = refs[-1]
    zi, xc = place_ref[0], place_ref[1]
    rows, cols, width = out_ref.shape
    groups = rows // SLAB
    octets = cols // SLAB
    for piece in range(2):
        for k in range(4):
            ref = refs[4 * piece + k]
            slabs = [
                ref[jnp.bitwise_xor(xc, o)].astype(F32).reshape(groups, SLAB, width) for o in range(octets)
            ]
            a = 4 * piece + jnp.bitwise_xor(zi, k)
            for m in range(groups):
                line = jnp.concatenate([slab[m] for slab in slabs], axis=0)
                out_ref[m * SLAB + a] = line.astype(BF16)


def gather(place, pieces, image):
    return pl.pallas_call(
        gather_kernel,
        in_specs=[SMEM] + [pl.BlockSpec(memory_space=pltpu.VMEM)] * 8,
        out_specs=pl.BlockSpec(memory_space=pltpu.VMEM),
        out_shape=jax.ShapeDtypeStruct(image.shape, BF16),
        compiler_params=PARAMS,
        name="gather",
    )(place, *pieces)


def position_bias(rel_table, strips):
    side = GRID
    per_strip = side // strips
    ids = jnp.arange(side * side, dtype=jnp.int32)
    col_of = ids // side
    row_of = ids % side
    col_pair = col_of[None, :] - col_of[:, None] + side - 1
    row_pair = row_of[None, :] - row_of[:, None] + side - 1
    offset = row_pair * (2 * side - 1) + col_pair
    offset = jnp.concatenate([offset, offset], axis=1)
    entries = jnp.arange((2 * side - 1) ** 2, dtype=jnp.int32)
    onehot = (entries[:, None] == offset.reshape(-1)[None, :]).astype(F32)
    bias = jnp.dot(rel_table, onehot, precision=lax.Precision.HIGHEST, preferred_element_type=F32)
    return bias.reshape(rel_table.shape[0], side * side, 2 * side * side)


def local(
    image,
    bn_gain,
    bn_shift,
    w_expand,
    b_expand,
    w_depth,
    b_depth,
    w_project,
    b_project,
    attn_gain,
    attn_shift,
    w_qkv,
    w_out,
    rel_table,
    ffn_gain,
    ffn_shift,
    w_up,
    b_up,
    w_down,
    b_down,
):
    rows, cols, width = image.shape
    strips = lax.axis_size("strip")
    tiles = lax.axis_size("tile")
    col_groups = tiles // GRID
    assert strips == 2 and rows * strips == GRID * SLAB and cols == 4 * SLAB
    strip = lax.axis_index("strip")
    tile = lax.axis_index("tile")
    grid_col = tile // col_groups
    zi = grid_col // 2
    xc = (grid_col % 2) * strips + strip
    flags = [tile > 0, tile < tiles - 1, strip > 0, strip < strips - 1]
    place = jnp.stack([jnp.asarray(v, jnp.int32) for v in [zi, xc] + flags])

    def row(v):
        return v.reshape(1, -1)

    def exchange(value, mask):
        pairs = []
        for g in range(GRID):
            for c in range(col_groups):
                for s in range(strips):
                    member = (g * strips + s) ^ mask
                    source = (g * col_groups + c) * strips + s
                    target = ((member // strips) * col_groups + c) * strips + member % strips
                    pairs.append((source, target))
        return lax.ppermute(value, ("tile", "strip"), pairs)

    edge_row = lax.dynamic_index_in_dim(image, jnp.where(strip == 0, rows - 1, 0), 0, keepdims=False)
    beyond = lax.ppermute(edge_row, "strip", [(0, 1), (1, 0)])
    sides = edges(image, beyond, beyond)
    up_tile = [(i, (i + 1) % tiles) for i in range(tiles - 1)]
    down_tile = [(j, i) for i, j in up_tile]
    left = lax.ppermute(sides[1], "tile", up_tile)
    right = lax.ppermute(sides[0], "tile", down_tile)

    expand_weights = (row(bn_gain), row(bn_shift), w_expand, row(b_expand))
    expanded = expand(image.reshape(rows * cols, width), *expand_weights).reshape(rows, cols, -1)
    conv_weights = expand_weights + (w_depth, row(b_depth), w_project, row(b_project))
    bias = position_bias(rel_table, strips)
    attend_weights = (
        row(attn_gain),
        row(attn_shift),
        w_qkv,
        w_out,
        bias,
        row(ffn_gain),
        row(ffn_shift),
        w_up,
        row(b_up),
        w_down,
        row(b_down),
    )

    pieces = []
    for piece in range(2):
        sections = conv(piece, place, expanded, image, left, right, beyond, beyond, conv_weights)
        near = [sections[0]] + [exchange(sections[k], 4 * k) for k in range(1, 4)]
        arrived = []
        for j in range(4):
            block = jnp.stack([near[k][j] for k in range(4)])
            arrived.append(exchange(block, j) if j else block)
        results = attend(place, arrived, rel_table.shape[0], attend_weights)
        back = [results[0]] + [exchange(results[j], j) for j in range(1, 4)]
        for k in range(4):
            block = jnp.stack([back[j][k] for j in range(4)])
            pieces.append(exchange(block, 4 * k) if k else block)
    return gather(place, pieces, image)


def solution(mesh):
    return jax.shard_map(
        local,
        mesh=mesh,
        in_specs=(P(("group", "strip"), "tile", None),) + (P(),) * 19,
        out_specs=P(("group", "strip"), "tile", None),
        check_vma=False,
    )
```

```python
import functools

import jax
import jax.numpy as jnp
from jax import lax
from jax.experimental import pallas as pl
from jax.experimental.pallas import tpu as pltpu
from jax.sharding import PartitionSpec as P

GRID = 8
EPSILON = 1e-05
F32 = jnp.float32
BF16 = jnp.bfloat16
SLAB = 8
ROW_GAIN, ROW_SHIFT, ROW_EXPAND, ROW_DEPTH, ROW_PROJECT, ROW_TAPS, ROWS = 0, 1, 2, 3, 4, 8, 24
LANES = 128
VMEM_LIMIT = 48 * 1024 * 1024


def dot(lhs, rhs):
    return jnp.dot(lhs, rhs, preferred_element_type=F32)


def dot_nt(lhs, rhs):
    return lax.dot_general(lhs, rhs, (((1,), (1,)), ((), ())), preferred_element_type=F32)


def gelu(v):
    half = 0.5 * v
    inner = v * (0.7978845608028654 + (0.7978845608028654 * 0.044715) * (v * v))
    return half + half * jnp.tanh(inner)


def layer_norm(x, gain, shift):
    center = jnp.mean(x, axis=-1, keepdims=True)
    diff = x - center
    spread = jnp.mean(diff * diff, axis=-1, keepdims=True)
    return diff * lax.rsqrt(spread + EPSILON) * gain + shift


def full(shape):
    return pl.BlockSpec(shape, lambda *_: (0,) * len(shape))


VMEM = pl.BlockSpec(memory_space=pltpu.VMEM)
ANY = pl.BlockSpec(memory_space=pl.ANY)
PARAMS = pltpu.CompilerParams(vmem_limit_bytes=VMEM_LIMIT)


class Place:
    def __init__(self):
        self.strips = lax.axis_size("strip")
        self.tiles = lax.axis_size("tile")
        self.col_groups = self.tiles // GRID
        self.strip = lax.axis_index("strip")
        self.tile = lax.axis_index("tile")
        grid_col = self.tile // self.col_groups
        self.zi = grid_col // 2
        self.xc = (grid_col % 2) * self.strips + self.strip
        self.odd = self.tile % 2


def split3(x):
    high = x.astype(BF16)
    rest = x - high.astype(F32)
    middle = rest.astype(BF16)
    return [high, middle, (rest - middle.astype(F32)).astype(BF16)]


def edges_kernel(image_ref, beyond_ref, even_ref, odd_ref):
    place = Place()
    rows, cols, width = image_ref.shape
    pixels = image_ref[...].reshape(rows * cols, width)
    pick = lax.broadcasted_iota(jnp.int32, (2 * rows, rows * cols), 0)
    where = lax.broadcasted_iota(jnp.int32, (2 * rows, rows * cols), 1)
    first, last = place.odd, 1 - place.odd
    wanted = jnp.where(
        pick < rows, pick * cols + last * (cols - 1), (pick - rows) * cols + first * (cols - 1)
    )
    onehot = jnp.where(where == wanted, 1.0, 0.0).astype(BF16)
    columns = dot(onehot, pixels)
    beyond = beyond_ref[...].astype(F32)
    corners = [jnp.broadcast_to(beyond[c : c + 1], (2 * SLAB, width)) for c in (0, cols - 1)]
    for side, ref in ((0, even_ref), (1, odd_ref)):
        outer = place.odd == side
        corner = jnp.where(outer, corners[1], corners[0])
        ref[...] = jnp.concatenate([columns[side * rows : (side + 1) * rows], corner], axis=0).astype(BF16)


def edges(image, beyond):
    rows, cols, width = image.shape
    return pl.pallas_call(
        edges_kernel,
        out_shape=[jax.ShapeDtypeStruct((rows + 2 * SLAB, width), BF16)] * 2,
        compiler_params=PARAMS,
        cost_estimate=pl.CostEstimate(flops=4_000_000_000, bytes_accessed=1_000_000, transcendentals=0),
        name="edges",
    )(image, beyond)


def table_kernel(rel_ref, out_ref, rel_pad_ref, flat_ref):
    heads, entries = rel_ref.shape
    span = 2 * GRID - 1
    depth = rel_pad_ref.shape[1]
    rel_pad_ref[...] = jnp.zeros_like(rel_pad_ref)
    rel_pad_ref[:, :entries] = rel_ref[...]
    parts = jnp.concatenate(split3(rel_pad_ref[...]), axis=0)
    entry = lax.broadcasted_iota(jnp.int32, (depth, LANES), 0)
    lane = lax.broadcasted_iota(jnp.int32, (depth, LANES), 1)
    wanted = (lane % GRID + GRID - 1) * span + lane // GRID
    for k in range(GRID):
        onehot = jnp.where(entry == wanted - k * span, 1.0, 0.0).astype(BF16)
        found = dot(parts, onehot)
        flat_ref[k * heads : (k + 1) * heads, :] = (
            found[:heads] + found[heads : 2 * heads] + found[2 * heads :]
        )
    for h in range(heads):
        out_ref[h] = flat_ref[pl.ds(h, GRID, stride=heads), :]


def table(rel_table):
    heads, entries = rel_table.shape
    depth = -(-entries // LANES) * LANES
    return pl.pallas_call(
        table_kernel,
        out_shape=jax.ShapeDtypeStruct((heads, GRID, LANES), F32),
        scratch_shapes=[pltpu.VMEM((heads, depth), F32), pltpu.VMEM((GRID * heads, LANES), F32)],
        compiler_params=PARAMS,
        name="table",
    )(rel_table)


def expand_block(pixels, gain, shift, w_ref, bias, store):
    normed = (pixels.astype(F32) * gain + shift).astype(BF16)
    step = 2 * LANES
    for n in range(w_ref.shape[1] // step):
        part = slice(n * step, (n + 1) * step)
        store(part, gelu(dot(normed, w_ref[:, part]) + bias[:, part]))


def expand_kernel(image_ref, w_ref, *refs):
    out_ref, vectors_ref = refs[-2:]
    width, hidden = w_ref.shape
    vectors_ref[...] = jnp.zeros_like(vectors_ref)
    for line, ref in zip((ROW_GAIN, ROW_SHIFT, ROW_EXPAND, ROW_DEPTH, ROW_PROJECT, ROW_TAPS), refs):
        vectors_ref[line : line + ref.shape[0], : ref.shape[1]] = ref[...]
    rows, cols, _ = image_ref.shape
    per = SLAB
    gain = vectors_ref[ROW_GAIN : ROW_GAIN + 1, :width]
    shift = vectors_ref[ROW_SHIFT : ROW_SHIFT + 1, :width]
    bias = vectors_ref[ROW_EXPAND : ROW_EXPAND + 1, :]

    def step(i, carry):
        spot = pl.ds(i * per, per)

        def store(part, value):
            out_ref[spot, :, part] = value.astype(BF16).reshape(per, cols, value.shape[-1])

        expand_block(image_ref[spot].reshape(per * cols, width), gain, shift, w_ref, bias, store)
        return carry

    lax.fori_loop(0, rows // per, step, 0)


def expand(image, w_expand, vectors):
    rows, cols, width = image.shape
    hidden = w_expand.shape[1]
    return pl.pallas_call(
        expand_kernel,
        in_specs=[VMEM] * (2 + len(vectors)),
        out_specs=[VMEM] * 2,
        out_shape=[
            jax.ShapeDtypeStruct((rows, cols, hidden), BF16),
            jax.ShapeDtypeStruct((ROWS, hidden), F32),
        ],
        compiler_params=PARAMS,
        cost_estimate=pl.CostEstimate(
            flops=16 * rows * cols * width * hidden, bytes_accessed=4_000_000, transcendentals=rows * cols * hidden
        ),
        name="expand",
    )(image, w_expand, *vectors)


def conv_kernel(
    piece,
    expanded_ref,
    image_ref,
    even_ref,
    odd_ref,
    outer_ref,
    w_expand_ref,
    w_project_ref,
    vectors_ref,
    out0_ref,
    out1_ref,
    out2_ref,
    out3_ref,
    rim_ref,
    side_ref,
    beyond_ref,
    tap_ref,
    deep_ref,
):
    place = Place()
    rows, cols, width = image_ref.shape
    hidden = expanded_ref.shape[-1]
    places = 4
    groups = rows // SLAB
    first = piece * places
    zi, xc = place.zi, place.xc

    def tap(t):
        return vectors_ref[ROW_TAPS + t : ROW_TAPS + t + 1, :]

    is_odd = place.odd == 1
    even, odd = even_ref[...].astype(F32), odd_ref[...].astype(F32)
    left, right = jnp.where(is_odd, even, odd), jnp.where(is_odd, odd, even)
    rim_in = jnp.concatenate([left, right, outer_ref[...].astype(F32)], axis=0)

    def store(part, value):
        rim_ref[:, part] = value.astype(BF16).astype(F32)

    expand_block(
        rim_in,
        vectors_ref[ROW_GAIN : ROW_GAIN + 1, :width],
        vectors_ref[ROW_SHIFT : ROW_SHIFT + 1, :width],
        w_expand_ref,
        vectors_ref[ROW_EXPAND : ROW_EXPAND + 1, :],
        store,
    )
    ok_left, ok_right = place.tile > 0, place.tile < place.tiles - 1
    ok_up, ok_down = place.strip > 0, place.strip < place.strips - 1
    ok_outer = ok_up if piece == 0 else ok_down
    tall = rows + 2 * SLAB
    beyond_ref[...] = jnp.where(ok_outer, rim_ref[2 * tall : 2 * tall + cols, :], 0.0).astype(BF16)
    for side, ok in ((0, ok_left), (1, ok_right)):
        base = side * tall
        corner = rim_ref[base + rows : base + rows + 1, :]
        side_ref[1 : rows + 1, :] = jnp.where(ok, rim_ref[base : base + rows, :], 0.0)
        side_ref[0:1, :] = jnp.where(jnp.logical_and(ok, ok_up), corner, 0.0)
        side_ref[rows + 1 : rows + 2, :] = jnp.where(jnp.logical_and(ok, ok_down), corner, 0.0)
        j = 2 * side
        tap_ref[side] = (
            side_ref[0:rows, :] * tap(j)
            + side_ref[1 : rows + 1, :] * tap(3 + j)
            + side_ref[2 : rows + 2, :] * tap(6 + j)
        )

    col_id = lax.broadcasted_iota(jnp.int32, (cols, LANES), 0)

    def chunk(index, carry):
        lanes = pl.ds(pl.multiple_of(index * LANES, LANES), LANES)
        weights = [vectors_ref[ROW_TAPS + t : ROW_TAPS + t + 1, lanes] for t in range(9)]
        bias = vectors_ref[ROW_DEPTH : ROW_DEPTH + 1, lanes]
        for m in range(groups):
            above = m * SLAB + first - 1
            lines = []
            for q in range(places + 2):
                r = above + q
                if 0 <= r < rows:
                    lines.append(expanded_ref[r, :, lanes].astype(F32))
                else:
                    lines.append(beyond_ref[:, lanes].astype(F32))
            for q in range(places):
                r = above + 1 + q
                sums = [
                    lines[q] * weights[j] + lines[q + 1] * weights[3 + j] + lines[q + 2] * weights[6 + j]
                    for j in range(3)
                ]
                before = jnp.where(col_id == 0, tap_ref[0, r : r + 1, lanes], pltpu.roll(sums[0], 1, 0))
                after = jnp.where(
                    col_id == cols - 1, tap_ref[1, r : r + 1, lanes], pltpu.roll(sums[2], cols - 1, 0)
                )
                deep_ref[q, m, :, lanes] = gelu(before + sums[1] + after + bias).astype(BF16)
        return carry

    lax.fori_loop(0, hidden // LANES, chunk, 0)

    octets = cols // SLAB
    b_project = vectors_ref[ROW_PROJECT : ROW_PROJECT + 1, :width]
    for k, out_ref in enumerate((out0_ref, out1_ref, out2_ref, out3_ref)):
        q = jnp.bitwise_xor(zi, k)
        projected = dot(deep_ref[q].reshape(groups * cols, hidden), w_project_ref[...]) + b_project
        own = jnp.stack([image_ref[m * SLAB + first + q] for m in range(groups)]).astype(F32)
        section = (own + projected.reshape(groups, cols, width)).reshape(groups, octets, SLAB, width)
        for o in range(octets):
            out_ref[jnp.bitwise_xor(xc, o)] = section[:, o].reshape(groups * SLAB, width).astype(BF16)


def conv(piece, expanded, image, even, odd, outer, w_expand, w_project, vectors):
    rows, cols, width = image.shape
    hidden = expanded.shape[-1]
    groups = rows // SLAB
    tall = rows + 2 * SLAB
    shape = jax.ShapeDtypeStruct((4, groups * SLAB, width), BF16)
    return pl.pallas_call(
        functools.partial(conv_kernel, piece),
        in_specs=[VMEM] * 8,
        out_specs=[VMEM] * 4,
        out_shape=[shape] * 4,
        scratch_shapes=[
            pltpu.VMEM((2 * tall + cols, hidden), F32),
            pltpu.VMEM((rows + SLAB, hidden), F32),
            pltpu.VMEM((cols, hidden), BF16),
            pltpu.VMEM((2, rows, hidden), F32),
            pltpu.VMEM((4, groups, cols, hidden), BF16),
        ],
        compiler_params=PARAMS,
        cost_estimate=pl.CostEstimate(
            flops=rows * cols * width * hidden, bytes_accessed=6_000_000, transcendentals=rows * cols * hidden
        ),
        name="conv",
    )(expanded, image, even, odd, outer, w_expand, w_project, vectors)


def attend_kernel(
    heads,
    in0_ref,
    in1_ref,
    in2_ref,
    in3_ref,
    gain_ref,
    shift_ref,
    w_qkv_ref,
    w_out_ref,
    table_ref,
    out0_ref,
    out1_ref,
    out2_ref,
    out3_ref,
    token_ref,
    normed_ref,
    query_t_ref,
    value_t_ref,
    bias_ref,
):
    place = Place()
    zi, xc = place.zi, place.xc
    halves, count, _ = normed_ref.shape
    width = halves * LANES
    chunk_rows = token_ref.shape[1]
    head = width // heads
    tokens = GRID * GRID
    wins = count // tokens

    for j, ref in enumerate((in0_ref, in1_ref, in2_ref, in3_ref)):
        for k in range(4):
            slot = jnp.bitwise_xor(zi, k) * 4 + jnp.bitwise_xor(xc, j)
            x = ref[k].astype(F32)
            token_ref[slot] = x
            normed = layer_norm(x, gain_ref[...], shift_ref[...])
            spot = pl.ds(pl.multiple_of(slot * chunk_rows, chunk_rows), chunk_rows)
            for c in range(halves):
                normed_ref[c, spot, :] = normed[:, c * LANES : (c + 1) * LANES]

    query_t_ref[...] = w_qkv_ref[:, :width].T
    value_t_ref[...] = w_qkv_ref[:, 2 * width :].T
    left_half = lax.broadcasted_iota(jnp.int32, (tokens, 2 * tokens), 1) < tokens
    row_head = lax.broadcasted_iota(jnp.int32, (LANES, 2 * tokens), 0) // head
    per_group = LANES // head

    lane_half = lax.broadcasted_iota(jnp.int32, (GRID, 2 * tokens), 1) < tokens
    for h in range(heads):
        base = table_ref[h]
        for c in range(GRID):
            off = (GRID - 1 - c) * GRID
            one = pltpu.roll(base, (LANES - off) % LANES, 1)
            two = pltpu.roll(base, (LANES - off + tokens) % LANES, 1)
            bias_ref[h, c * GRID : (c + 1) * GRID, :] = jnp.where(lane_half, one, two)

    for pair in range(wins // 2):
        spots = [pl.ds(2 * pair + w, tokens, stride=wins) for w in range(2)]
        columns = [jnp.concatenate([normed_ref[c, s, :] for s in spots], axis=0) for c in range(halves)]
        normed = jnp.concatenate(columns, axis=1).astype(BF16)
        keys = dot(normed, w_qkv_ref[:, width : 2 * width]).astype(BF16)
        query_t = (dot_nt(query_t_ref[...], normed) * head ** (-0.5)).astype(BF16)
        value_t = dot_nt(value_t_ref[...], normed).astype(BF16)
        parts = []
        for h in range(heads):
            g = h // per_group
            span = slice(g * LANES, (g + 1) * LANES)
            own = jnp.where(row_head == h % per_group, query_t[span], jnp.zeros((), BF16))
            both = dot(keys[:, span], own)
            scores = jnp.where(left_half, both[:tokens], both[tokens:]) + bias_ref[h]
            weight = jnp.exp(scores - jnp.max(scores, axis=0, keepdims=True))
            probs = weight * (1.0 / jnp.sum(weight, axis=0, keepdims=True))
            spread = jnp.concatenate(
                [jnp.where(left_half, probs, 0.0), jnp.where(left_half, 0.0, probs)], axis=0
            ).astype(BF16)
            parts.append(dot(value_t[h * head : (h + 1) * head], spread))
        context = jnp.concatenate(parts, axis=0).astype(BF16).T
        attended = dot(context, w_out_ref[...])
        for w, spot in enumerate(spots):
            for c in range(halves):
                normed_ref[c, spot, :] = attended[w * tokens : (w + 1) * tokens, c * LANES : (c + 1) * LANES]

    for j, ref in enumerate((out0_ref, out1_ref, out2_ref, out3_ref)):
        for k in range(4):
            slot = jnp.bitwise_xor(zi, k) * 4 + jnp.bitwise_xor(xc, j)
            spot = pl.ds(pl.multiple_of(slot * chunk_rows, chunk_rows), chunk_rows)
            added = jnp.concatenate([normed_ref[c, spot, :] for c in range(halves)], axis=1)
            ref[k] = (token_ref[slot] + added).astype(BF16)


def attend(arrived, heads, weights):
    chunk_rows, width = arrived[0].shape[1:]
    count = 16 * chunk_rows
    flops = 2 * count * width * (4 * width)
    tokens = GRID * GRID
    shape = jax.ShapeDtypeStruct(arrived[0].shape, BF16)
    return pl.pallas_call(
        functools.partial(attend_kernel, heads),
        in_specs=[VMEM] * 9,
        out_specs=[VMEM] * 4,
        out_shape=[shape] * 4,
        scratch_shapes=[
            pltpu.VMEM((16, chunk_rows, width), F32),
            pltpu.VMEM((width // LANES, count, LANES), F32),
            pltpu.VMEM((width, width), BF16),
            pltpu.VMEM((width, width), BF16),
            pltpu.VMEM((heads, tokens, 2 * tokens), F32),
        ],
        compiler_params=PARAMS,
        cost_estimate=pl.CostEstimate(flops=flops, bytes_accessed=4_000_000, transcendentals=count * 512),
        name="attend",
    )(*arrived, *weights)


def feed_kernel(piece, *refs):
    in_refs = refs[:4]
    gain_ref, shift_ref, w_up_ref, b_up_ref, w_down_ref, b_down_ref = refs[4:10]
    out_ref, line_ref, sems = refs[-3:]
    place = Place()
    zi, xc = place.zi, place.xc
    groups, places, cols, width = line_ref.shape
    octets = cols // SLAB
    step = 2 * LANES
    for k, ref in enumerate(in_refs):
        slabs = [ref[jnp.bitwise_xor(xc, o)].astype(F32).reshape(groups, 1, SLAB, width) for o in range(octets)]
        section = jnp.concatenate(slabs, axis=1).reshape(groups * cols, width)
        normed = layer_norm(section, gain_ref[...], shift_ref[...]).astype(BF16)
        total = section + b_down_ref[...]
        for n in range(w_up_ref.shape[1] // step):
            inner = slice(n * step, (n + 1) * step)
            hidden = gelu(dot(normed, w_up_ref[:, inner]) + b_up_ref[:, inner]).astype(BF16)
            total = total + dot(hidden, w_down_ref[inner, :])
        result = total.reshape(groups, cols, width).astype(BF16)
        a = jnp.bitwise_xor(zi, k)
        for m in range(groups):
            line_ref[m, a] = result[m]
    copies = [
        pltpu.make_async_copy(
            line_ref.at[m], out_ref.at[pl.ds(m * SLAB + piece * places, places)], sems.at[m]
        )
        for m in range(groups)
    ]
    for copy in copies:
        copy.start()
    for copy in copies:
        copy.wait()


def feed(piece, sections, weights, image, partial):
    rows, cols, width = image.shape
    groups = rows // SLAB
    hidden = weights[2].shape[1]
    count = rows * cols // 2
    extra = [] if partial is None else [partial]
    return pl.pallas_call(
        functools.partial(feed_kernel, piece),
        in_specs=[VMEM] * 10 + [ANY] * len(extra),
        out_specs=ANY,
        out_shape=jax.ShapeDtypeStruct(image.shape, BF16),
        scratch_shapes=[pltpu.VMEM((groups, 4, cols, width), BF16), pltpu.SemaphoreType.DMA((groups,))],
        input_output_aliases={10: 0} if extra else {},
        compiler_params=PARAMS,
        cost_estimate=pl.CostEstimate(
            flops=4 * count * width * hidden, bytes_accessed=2_000_000, transcendentals=count * hidden
        ),
        name="feed",
    )(*sections, *weights, *extra)


def local(
    image,
    bn_gain,
    bn_shift,
    w_expand,
    b_expand,
    w_depth,
    b_depth,
    w_project,
    b_project,
    attn_gain,
    attn_shift,
    w_qkv,
    w_out,
    rel_table,
    ffn_gain,
    ffn_shift,
    w_up,
    b_up,
    w_down,
    b_down,
):
    rows, cols, width = image.shape
    strips = lax.axis_size("strip")
    tiles = lax.axis_size("tile")
    col_groups = tiles // GRID
    assert strips == 2 and rows * strips == GRID * SLAB and cols == 4 * SLAB
    strip = lax.axis_index("strip")

    def row(v):
        return v.reshape(1, -1)

    def exchange(value, mask):
        pairs = []
        for g in range(GRID):
            for c in range(col_groups):
                for s in range(strips):
                    member = (g * strips + s) ^ mask
                    source = (g * col_groups + c) * strips + s
                    target = ((member // strips) * col_groups + c) * strips + member % strips
                    pairs.append((source, target))
        return lax.ppermute(value, ("tile", "strip"), pairs)

    edge_row = lax.dynamic_index_in_dim(image, jnp.where(strip == 0, rows - 1, 0), 0, keepdims=False)
    beyond = lax.ppermute(edge_row, "strip", [(0, 1), (1, 0)])
    to_even, to_odd = edges(image, beyond)
    even_pairs = [(i, i ^ 1) for i in range(tiles)]
    odd_pairs = [(i, i + 1) for i in range(1, tiles - 1, 2)]
    odd_pairs = odd_pairs + [(j, i) for i, j in odd_pairs]
    even = lax.ppermute(to_even, "tile", even_pairs)
    odd = lax.ppermute(to_odd, "tile", odd_pairs)

    vectors_in = (row(bn_gain), row(bn_shift), row(b_expand), row(b_depth), row(b_project), w_depth)
    expanded, vectors = expand(image, w_expand, vectors_in)
    attend_weights = (row(attn_gain), row(attn_shift), w_qkv, w_out, table(rel_table))
    feed_weights = (row(ffn_gain), row(ffn_shift), w_up, row(b_up), w_down, row(b_down))
    heads = rel_table.shape[0]

    def sections_of(piece):
        return conv(piece, expanded, image, even, odd, beyond, w_expand, w_project, vectors)

    def along_z(blocks):
        return [blocks[0]] + [exchange(blocks[k], 4 * k) for k in range(1, 4)]

    def regroup(blocks):
        return [jnp.stack([blocks[k][j] for k in range(4)]) for j in range(4)]

    def within(blocks):
        return [blocks[0]] + [exchange(blocks[j], j) for j in range(1, 4)]

    def after(first, then):
        return lax.optimization_barrier((first, then))

    near_a = along_z(sections_of(0))
    sections_b = sections_of(1)
    near_a, sections_b = after(near_a, sections_b)
    held_a = within(regroup(near_a))
    held_a[1], sections_b = after(held_a[1], sections_b)
    near_b = along_z(sections_b)
    results_a = attend(held_a, heads, attend_weights)
    near_b, results_a = after(near_b, results_a)
    held_b = within(regroup(near_b))
    held_b[1], results_a = after(held_b[1], results_a)
    done_a = within(results_a)
    results_b = attend(held_b, heads, attend_weights)
    done_a, results_b = after(done_a, results_b)
    done_b = within(results_b)
    back_a = regroup(done_a)
    done_b[1], back_a = after(done_b[1], back_a)
    home_a = along_z(back_a)
    home_b = along_z(regroup(done_b))
    out = feed(0, home_a, feed_weights, image, None)
    return feed(1, home_b, feed_weights, image, out)


def solution(mesh):
    return jax.shard_map(
        local,
        mesh=mesh,
        in_specs=(P(("group", "strip"), "tile", None),) + (P(),) * 19,
        out_specs=P(("group", "strip"), "tile", None),
        check_vma=False,
    )
```

```python
import functools

import jax
import jax.numpy as jnp
from jax import lax
from jax.experimental import pallas as pl
from jax.experimental.pallas import tpu as pltpu
from jax.sharding import PartitionSpec as P

GRID = 8
EPSILON = 1e-05
F32 = jnp.float32
BF16 = jnp.bfloat16
SLAB = 8
ROW_GAIN, ROW_SHIFT, ROW_EXPAND, ROW_DEPTH, ROW_PROJECT, ROW_TAPS, ROWS = 0, 1, 2, 3, 4, 8, 24
LANES = 128
VMEM_LIMIT = 48 * 1024 * 1024


def dot(lhs, rhs):
    return jnp.dot(lhs, rhs, preferred_element_type=F32)


def dot_nt(lhs, rhs):
    return lax.dot_general(lhs, rhs, (((1,), (1,)), ((), ())), preferred_element_type=F32)


def gelu(v):
    half = 0.5 * v
    inner = v * (0.7978845608028654 + (0.7978845608028654 * 0.044715) * (v * v))
    return half + half * jnp.tanh(inner)


def layer_norm(x, gain, shift):
    center = jnp.mean(x, axis=-1, keepdims=True)
    diff = x - center
    spread = jnp.mean(diff * diff, axis=-1, keepdims=True)
    return diff * lax.rsqrt(spread + EPSILON) * gain + shift


def full(shape):
    return pl.BlockSpec(shape, lambda *_: (0,) * len(shape))


VMEM = pl.BlockSpec(memory_space=pltpu.VMEM)
ANY = pl.BlockSpec(memory_space=pl.ANY)
PARAMS = pltpu.CompilerParams(vmem_limit_bytes=VMEM_LIMIT)


class Place:
    def __init__(self):
        self.strips = lax.axis_size("strip")
        self.tiles = lax.axis_size("tile")
        self.col_groups = self.tiles // GRID
        self.strip = lax.axis_index("strip")
        self.tile = lax.axis_index("tile")
        grid_col = self.tile // self.col_groups
        self.zi = grid_col // 2
        self.xc = (grid_col % 2) * self.strips + self.strip
        self.odd = self.tile % 2


def split3(x):
    high = x.astype(BF16)
    rest = x - high.astype(F32)
    middle = rest.astype(BF16)
    return [high, middle, (rest - middle.astype(F32)).astype(BF16)]


def border_kernel(image_ref, out_ref):
    out_ref[...] = image_ref[jnp.where(Place().strip == 0, image_ref.shape[0] - 1, 0)]


def border(image):
    return pl.pallas_call(
        border_kernel,
        in_specs=[VMEM],
        out_specs=VMEM,
        out_shape=jax.ShapeDtypeStruct(image.shape[1:], BF16),
        compiler_params=PARAMS,
        name="border",
    )(image)


def edges_kernel(image_ref, beyond_ref, even_ref, odd_ref):
    place = Place()
    rows, cols, width = image_ref.shape
    pixels = image_ref[...].reshape(rows * cols, width)
    pick = lax.broadcasted_iota(jnp.int32, (2 * rows, rows * cols), 0)
    where = lax.broadcasted_iota(jnp.int32, (2 * rows, rows * cols), 1)
    first, last = place.odd, 1 - place.odd
    wanted = jnp.where(
        pick < rows, pick * cols + last * (cols - 1), (pick - rows) * cols + first * (cols - 1)
    )
    onehot = jnp.where(where == wanted, 1.0, 0.0).astype(BF16)
    columns = dot(onehot, pixels)
    beyond = beyond_ref[...].astype(F32)
    corners = [jnp.broadcast_to(beyond[c : c + 1], (2 * SLAB, width)) for c in (0, cols - 1)]
    for side, ref in ((0, even_ref), (1, odd_ref)):
        outer = place.odd == side
        corner = jnp.where(outer, corners[1], corners[0])
        ref[...] = jnp.concatenate([columns[side * rows : (side + 1) * rows], corner], axis=0).astype(BF16)


def edges(image, beyond):
    rows, cols, width = image.shape
    return pl.pallas_call(
        edges_kernel,
        out_shape=[jax.ShapeDtypeStruct((rows + 2 * SLAB, width), BF16)] * 2,
        compiler_params=PARAMS,
        cost_estimate=pl.CostEstimate(flops=4_000_000_000, bytes_accessed=1_000_000, transcendentals=0),
        name="edges",
    )(image, beyond)


def table_kernel(rel_ref, out_ref, rel_pad_ref, flat_ref):
    heads, entries = rel_ref.shape
    span = 2 * GRID - 1
    depth = rel_pad_ref.shape[1]
    rel_pad_ref[...] = jnp.zeros_like(rel_pad_ref)
    rel_pad_ref[:, :entries] = rel_ref[...]
    parts = jnp.concatenate(split3(rel_pad_ref[...]), axis=0)
    entry = lax.broadcasted_iota(jnp.int32, (depth, LANES), 0)
    lane = lax.broadcasted_iota(jnp.int32, (depth, LANES), 1)
    wanted = (lane % GRID + GRID - 1) * span + lane // GRID
    for k in range(GRID):
        onehot = jnp.where(entry == wanted - k * span, 1.0, 0.0).astype(BF16)
        found = dot(parts, onehot)
        flat_ref[k * heads : (k + 1) * heads, :] = (
            found[:heads] + found[heads : 2 * heads] + found[2 * heads :]
        )
    for h in range(heads):
        out_ref[h] = flat_ref[pl.ds(h, GRID, stride=heads), :]


def table(rel_table):
    heads, entries = rel_table.shape
    depth = -(-entries // LANES) * LANES
    return pl.pallas_call(
        table_kernel,
        out_shape=jax.ShapeDtypeStruct((heads, GRID, LANES), F32),
        scratch_shapes=[pltpu.VMEM((heads, depth), F32), pltpu.VMEM((GRID * heads, LANES), F32)],
        compiler_params=PARAMS,
        name="table",
    )(rel_table)


def expand_block(pixels, gain, shift, w_ref, bias, store):
    normed = (pixels.astype(F32) * gain + shift).astype(BF16)
    step = 2 * LANES
    for n in range(w_ref.shape[1] // step):
        part = slice(n * step, (n + 1) * step)
        store(part, gelu(dot(normed, w_ref[:, part]) + bias[:, part]))


def expand_kernel(image_ref, w_ref, *refs):
    out_ref, vectors_ref = refs[-2:]
    width, hidden = w_ref.shape
    vectors_ref[...] = jnp.zeros_like(vectors_ref)
    for line, ref in zip((ROW_GAIN, ROW_SHIFT, ROW_EXPAND, ROW_DEPTH, ROW_PROJECT, ROW_TAPS), refs):
        vectors_ref[line : line + ref.shape[0], : ref.shape[1]] = ref[...]
    rows, cols, _ = image_ref.shape
    gain = vectors_ref[ROW_GAIN : ROW_GAIN + 1, :width]
    shift = vectors_ref[ROW_SHIFT : ROW_SHIFT + 1, :width]

    def store(part, value):
        out_ref[:, :, part] = value.astype(BF16).reshape(rows, cols, value.shape[-1])

    pixels = image_ref[...].reshape(rows * cols, width)
    expand_block(pixels, gain, shift, w_ref, vectors_ref[ROW_EXPAND : ROW_EXPAND + 1, :], store)


def expand(image, w_expand, vectors):
    rows, cols, width = image.shape
    hidden = w_expand.shape[1]
    return pl.pallas_call(
        expand_kernel,
        in_specs=[VMEM] * (2 + len(vectors)),
        out_specs=[VMEM] * 2,
        out_shape=[
            jax.ShapeDtypeStruct((rows, cols, hidden), BF16),
            jax.ShapeDtypeStruct((ROWS, hidden), F32),
        ],
        compiler_params=PARAMS,
        cost_estimate=pl.CostEstimate(
            flops=16 * rows * cols * width * hidden, bytes_accessed=4_000_000, transcendentals=rows * cols * hidden
        ),
        name="expand",
    )(image, w_expand, *vectors)


def rim_kernel(even_ref, odd_ref, outer_ref, w_expand_ref, vectors_ref, tap_ref, beyond_ref, rim_ref, side_ref):
    place = Place()
    cols, width = outer_ref.shape
    rows = tap_ref.shape[1]

    def tap(t):
        return vectors_ref[ROW_TAPS + t : ROW_TAPS + t + 1, :]

    is_odd = place.odd == 1
    even, odd = even_ref[...].astype(F32), odd_ref[...].astype(F32)
    left, right = jnp.where(is_odd, even, odd), jnp.where(is_odd, odd, even)
    rim_in = jnp.concatenate([left, right, outer_ref[...].astype(F32)], axis=0)

    def store(part, value):
        rim_ref[:, part] = value.astype(BF16).astype(F32)

    expand_block(
        rim_in,
        vectors_ref[ROW_GAIN : ROW_GAIN + 1, :width],
        vectors_ref[ROW_SHIFT : ROW_SHIFT + 1, :width],
        w_expand_ref,
        vectors_ref[ROW_EXPAND : ROW_EXPAND + 1, :],
        store,
    )
    ok_up, ok_down = place.strip > 0, place.strip < place.strips - 1
    tall = rows + 2 * SLAB
    beyond_ref[...] = rim_ref[2 * tall : 2 * tall + cols, :].astype(BF16)
    for side, ok in ((0, place.tile > 0), (1, place.tile < place.tiles - 1)):
        base = side * tall
        corner = rim_ref[base + rows : base + rows + 1, :]
        side_ref[1 : rows + 1, :] = jnp.where(ok, rim_ref[base : base + rows, :], 0.0)
        side_ref[0:1, :] = jnp.where(jnp.logical_and(ok, ok_up), corner, 0.0)
        side_ref[rows + 1 : rows + 2, :] = jnp.where(jnp.logical_and(ok, ok_down), corner, 0.0)
        j = 2 * side
        tap_ref[side] = (
            side_ref[0:rows, :] * tap(j)
            + side_ref[1 : rows + 1, :] * tap(3 + j)
            + side_ref[2 : rows + 2, :] * tap(6 + j)
        )


def rim(rows, even, odd, outer, w_expand, vectors):
    hidden = w_expand.shape[1]
    cols = outer.shape[0]
    return pl.pallas_call(
        rim_kernel,
        in_specs=[VMEM] * 5,
        out_specs=[VMEM] * 2,
        out_shape=[
            jax.ShapeDtypeStruct((2, rows, hidden), F32),
            jax.ShapeDtypeStruct((cols, hidden), BF16),
        ],
        scratch_shapes=[
            pltpu.VMEM((2 * even.shape[0] + cols, hidden), F32),
            pltpu.VMEM((rows + SLAB, hidden), F32),
        ],
        compiler_params=PARAMS,
        cost_estimate=pl.CostEstimate(
            flops=2 * 4 * cols * outer.shape[1] * hidden, bytes_accessed=1_000_000, transcendentals=4 * cols * hidden
        ),
        name="rim",
    )(even, odd, outer, w_expand, vectors)


def conv_kernel(
    far,
    expanded_ref,
    image_ref,
    tap_ref,
    outer_ref,
    w_project_ref,
    vectors_ref,
    own_ref,
    core_ref,
    section_ref,
    deep_ref,
):
    place = Place()
    rows, cols, width = image_ref.shape
    hidden = expanded_ref.shape[-1]
    groups = rows // SLAB
    octets = cols // SLAB
    half = SLAB // 2
    zi, xc = place.zi, place.xc
    pair = jnp.bitwise_xor(zi // 2, far) * 2
    at_top = pair == 0
    ok_up, ok_down = place.strip > 0, place.strip < place.strips - 1
    slab_id = lax.broadcasted_iota(jnp.int32, (SLAB, LANES), 0)

    def chunk(index, carry):
        lanes = pl.ds(pl.multiple_of(index * LANES, LANES), LANES)
        weights = [vectors_ref[ROW_TAPS + t : ROW_TAPS + t + 1, lanes] for t in range(9)]
        bias = vectors_ref[ROW_DEPTH : ROW_DEPTH + 1, lanes]
        outer = outer_ref[:, lanes].astype(F32)
        above_all = jnp.where(ok_up, outer, 0.0)
        below_all = jnp.where(ok_down, outer, 0.0)
        for m in range(groups):
            for p in range(2):
                start = m * SLAB + p * half + pair
                lines = []
                for q in range(4):
                    r = start + q - 1
                    if m == 0 and p == 0 and q == 0:
                        inside = expanded_ref[jnp.maximum(r, 0), :, lanes].astype(F32)
                        lines.append(jnp.where(at_top, above_all, inside))
                    elif m == groups - 1 and p == 1 and q == 3:
                        inside = expanded_ref[jnp.minimum(r, rows - 1), :, lanes].astype(F32)
                        lines.append(jnp.where(at_top, inside, below_all))
                    else:
                        lines.append(expanded_ref[r, :, lanes].astype(F32))
                for i in range(2):
                    sums = [
                        lines[i] * weights[j] + lines[i + 1] * weights[3 + j] + lines[i + 2] * weights[6 + j]
                        for j in range(3)
                    ]
                    within = p * half + pair + i
                    left = pltpu.roll(tap_ref[0, m * SLAB : (m + 1) * SLAB, lanes], (SLAB - within) % SLAB, 0)
                    right = pltpu.roll(tap_ref[1, m * SLAB : (m + 1) * SLAB, lanes], SLAB - 1 - within, 0)
                    before, after = pltpu.roll(sums[0], 1, 0), pltpu.roll(sums[2], cols - 1, 0)
                    head = jnp.where(slab_id == 0, left, before[:SLAB])
                    tail = jnp.where(slab_id == SLAB - 1, right, after[-SLAB:])
                    before = jnp.concatenate([head, before[SLAB:]], axis=0)
                    after = jnp.concatenate([after[:-SLAB], tail], axis=0)
                    deep_ref[p, i, m, :, lanes] = gelu(before + sums[1] + after + bias).astype(BF16)
        return carry

    lax.fori_loop(0, hidden // LANES, chunk, 0)

    b_project = vectors_ref[ROW_PROJECT : ROW_PROJECT + 1, :width]
    for k in range(2):
        i = jnp.bitwise_xor(zi % 2, k)
        for p in range(2):
            projected = dot(deep_ref[p, i].reshape(groups * cols, hidden), w_project_ref[...]) + b_project
            own = jnp.stack([image_ref[m * SLAB + p * half + pair + i] for m in range(groups)]).astype(F32)
            section = (own + projected.reshape(groups, cols, width)).reshape(groups, octets, SLAB, width)
            for o in range(octets):
                section_ref[k, p, o] = section[:, o].reshape(groups * SLAB, width)
            for j in range(4):
                ref = core_ref if j % 2 else own_ref
                ref[k, j // 2, p] = section_ref[k, p, jnp.bitwise_xor(xc, j)].astype(BF16)


def conv(far, expanded, image, taps, outer, w_project, vectors):
    rows, cols, width = image.shape
    hidden = expanded.shape[-1]
    groups = rows // SLAB
    octets = cols // SLAB
    shape = jax.ShapeDtypeStruct((2, 2, 2, groups * SLAB, width), BF16)
    return pl.pallas_call(
        functools.partial(conv_kernel, far),
        in_specs=[VMEM] * 6,
        out_specs=[VMEM] * 2,
        out_shape=[shape] * 2,
        scratch_shapes=[
            pltpu.VMEM((2, 2, octets, groups * SLAB, width), F32),
            pltpu.VMEM((2, 2, groups, cols, hidden), BF16),
        ],
        compiler_params=PARAMS,
        cost_estimate=pl.CostEstimate(
            flops=rows * cols * width * hidden, bytes_accessed=6_000_000, transcendentals=rows * cols * hidden
        ),
        name="conv",
    )(expanded, image, taps, outer, w_project, vectors)


def attend_kernel(heads, *refs):
    in_refs, refs = refs[:8], refs[8:]
    gain_ref, shift_ref, w_qkv_ref, w_out_ref, table_ref, own_ref, core_ref = refs[:7]
    token_ref, normed_ref, query_t_ref, value_t_ref, bias_ref, window_ref, key_ref, qt_ref, vt_ref, context_ref = refs[7:]
    place = Place()
    zi, xc = place.zi, place.xc
    halves, count, _ = normed_ref.shape
    width = halves * LANES
    chunk_rows = token_ref.shape[2]
    head = width // heads
    tokens = GRID * GRID
    wins = chunk_rows // 4
    sources = tokens // 4

    def spot_of(p, slot):
        return pl.ds(pl.multiple_of((p * sources + slot) * chunk_rows, chunk_rows), chunk_rows)

    def slot_of(k, j):
        return jnp.bitwise_xor(zi, k) * 4 + jnp.bitwise_xor(xc, j)

    for k in range(4):
        for j in range(4):
            slot = slot_of(k, j)
            for p in range(2):
                x = in_refs[2 * k + j // 2][j % 2, p].astype(F32)
                token_ref[p, slot] = x
                normed = layer_norm(x, gain_ref[...], shift_ref[...])
                for c in range(halves):
                    normed_ref[c, spot_of(p, slot), :] = normed[:, c * LANES : (c + 1) * LANES]

    query_t_ref[...] = w_qkv_ref[:, :width].T
    value_t_ref[...] = w_qkv_ref[:, 2 * width :].T
    left_half = lax.broadcasted_iota(jnp.int32, (tokens, 2 * tokens), 1) < tokens
    row_head = lax.broadcasted_iota(jnp.int32, (LANES, 2 * tokens), 0) // head
    per_group = LANES // head

    lane_half = lax.broadcasted_iota(jnp.int32, (GRID, 2 * tokens), 1) < tokens
    for h in range(heads):
        base = table_ref[h]
        for c in range(GRID):
            off = (GRID - 1 - c) * GRID
            one = pltpu.roll(base, (LANES - off) % LANES, 1)
            two = pltpu.roll(base, (LANES - off + tokens) % LANES, 1)
            bias_ref[h, c * GRID : (c + 1) * GRID, :] = jnp.where(lane_half, one, two)

    def window(win):
        return pl.ds((win // wins) * tokens * wins + win % wins, tokens, stride=wins)

    for win in range(2 * wins):
        picked = [normed_ref[c, window(win), :] for c in range(halves)]
        window_ref[win * tokens : (win + 1) * tokens, :] = jnp.concatenate(picked, axis=1).astype(BF16)
    normed = window_ref[...]
    key_ref[...] = dot(normed, w_qkv_ref[:, width : 2 * width]).astype(BF16)
    qt_ref[...] = (dot_nt(query_t_ref[...], normed) * head ** (-0.5)).astype(BF16)
    vt_ref[...] = dot_nt(value_t_ref[...], normed).astype(BF16)

    for pair in range(wins):
        lanes = slice(pair * 2 * tokens, (pair + 1) * 2 * tokens)
        for h in range(heads):
            g = h // per_group
            span = slice(g * LANES, (g + 1) * LANES)
            own = jnp.where(row_head == h % per_group, qt_ref[span, lanes], jnp.zeros((), BF16))
            both = dot(key_ref[lanes, span], own)
            scores = jnp.where(left_half, both[:tokens], both[tokens:]) + bias_ref[h]
            weight = jnp.exp(scores - jnp.max(scores, axis=0, keepdims=True))
            probs = weight * (1.0 / jnp.sum(weight, axis=0, keepdims=True))
            spread = jnp.concatenate(
                [jnp.where(left_half, probs, 0.0), jnp.where(left_half, 0.0, probs)], axis=0
            ).astype(BF16)
            context_ref[h * head : (h + 1) * head, lanes] = dot(vt_ref[h * head : (h + 1) * head, lanes], spread)
    context = context_ref[...].T.astype(BF16)
    attended = dot(context, w_out_ref[...])
    for win in range(2 * wins):
        for c in range(halves):
            normed_ref[c, window(win), :] = attended[
                win * tokens : (win + 1) * tokens, c * LANES : (c + 1) * LANES
            ]

    for k in range(4):
        for j in range(4):
            slot = slot_of(k, j)
            ref = core_ref if j % 2 else own_ref
            for p in range(2):
                added = jnp.concatenate([normed_ref[c, spot_of(p, slot), :] for c in range(halves)], axis=1)
                ref[k, j // 2, p] = (token_ref[p, slot] + added).astype(BF16)


def attend(arrived, heads, weights):
    chunk_rows, width = arrived[0].shape[2:]
    count = 32 * chunk_rows
    flops = 2 * count * width * (4 * width)
    tokens = GRID * GRID
    shape = jax.ShapeDtypeStruct((4, 2, 2, chunk_rows, width), BF16)
    return pl.pallas_call(
        functools.partial(attend_kernel, heads),
        in_specs=[VMEM] * 13,
        out_specs=[VMEM] * 2,
        out_shape=[shape] * 2,
        scratch_shapes=[
            pltpu.VMEM((2, 16, chunk_rows, width), F32),
            pltpu.VMEM((width // LANES, count, LANES), F32),
            pltpu.VMEM((width, width), BF16),
            pltpu.VMEM((width, width), BF16),
            pltpu.VMEM((heads, tokens, 2 * tokens), F32),
            pltpu.VMEM((count, width), BF16),
            pltpu.VMEM((count, width), BF16),
            pltpu.VMEM((width, count), BF16),
            pltpu.VMEM((width, count), BF16),
            pltpu.VMEM((width, count), F32),
        ],
        compiler_params=PARAMS,
        cost_estimate=pl.CostEstimate(flops=flops, bytes_accessed=4_000_000, transcendentals=count * 512),
        name="attend",
    )(*arrived, *weights)


def feed_kernel(far, *refs):
    in_refs, refs = refs[:4], refs[4:]
    gain_ref, shift_ref, w_up_ref, b_up_ref, w_down_ref, b_down_ref = refs[:6]
    out_ref, line_ref, section_ref, sems = refs[-4:]
    place = Place()
    zi, xc = place.zi, place.xc
    groups, _, _, cols, width = line_ref.shape
    half = SLAB // 2
    pair = jnp.bitwise_xor(zi // 2, far) * 2
    step = 2 * LANES
    for k in range(2):
        i = jnp.bitwise_xor(zi % 2, k)
        for p in range(2):
            for j in range(4):
                o = jnp.bitwise_xor(xc, j)
                section_ref[k, p, o] = in_refs[2 * k + j // 2][j % 2, p].astype(F32)
            slabs = [section_ref[k, p, o].reshape(groups, 1, SLAB, width) for o in range(cols // SLAB)]
            section = jnp.concatenate(slabs, axis=1).reshape(groups * cols, width)
            normed = layer_norm(section, gain_ref[...], shift_ref[...]).astype(BF16)
            total = section + b_down_ref[...]
            for n in range(w_up_ref.shape[1] // step):
                inner = slice(n * step, (n + 1) * step)
                hidden = gelu(dot(normed, w_up_ref[:, inner]) + b_up_ref[:, inner]).astype(BF16)
                total = total + dot(hidden, w_down_ref[inner, :])
            result = total.reshape(groups, cols, width).astype(BF16)
            for m in range(groups):
                line_ref[m, p, i] = result[m]
    copies = [
        pltpu.make_async_copy(
            line_ref.at[m, p], out_ref.at[pl.ds(m * SLAB + p * half + pair, 2)], sems.at[2 * m + p]
        )
        for m in range(groups)
        for p in range(2)
    ]
    for copy in copies:
        copy.start()
    for copy in copies:
        copy.wait()


def feed(far, sections, weights, image, partial):
    rows, cols, width = image.shape
    groups = rows // SLAB
    hidden = weights[2].shape[1]
    count = rows * cols // 2
    extra = [] if partial is None else [partial]
    return pl.pallas_call(
        functools.partial(feed_kernel, far),
        in_specs=[VMEM] * 10 + [ANY] * len(extra),
        out_specs=ANY,
        out_shape=jax.ShapeDtypeStruct(image.shape, BF16),
        scratch_shapes=[
            pltpu.VMEM((groups, 2, 2, cols, width), BF16),
            pltpu.VMEM((2, 2, cols // SLAB, groups * SLAB, width), F32),
            pltpu.SemaphoreType.DMA((2 * groups,)),
        ],
        input_output_aliases={10: 0} if extra else {},
        compiler_params=PARAMS,
        cost_estimate=pl.CostEstimate(
            flops=4 * count * width * hidden, bytes_accessed=2_000_000, transcendentals=count * hidden
        ),
        name="feed",
    )(*sections, *weights, *extra)


def local(
    image,
    bn_gain,
    bn_shift,
    w_expand,
    b_expand,
    w_depth,
    b_depth,
    w_project,
    b_project,
    attn_gain,
    attn_shift,
    w_qkv,
    w_out,
    rel_table,
    ffn_gain,
    ffn_shift,
    w_up,
    b_up,
    w_down,
    b_down,
):
    rows, cols, width = image.shape
    strips = lax.axis_size("strip")
    tiles = lax.axis_size("tile")
    col_groups = tiles // GRID
    assert strips == 2 and rows * strips == GRID * SLAB and cols == 4 * SLAB

    def row(v):
        return v.reshape(1, -1)

    def exchange(value, mask):
        pairs = []
        for g in range(GRID):
            for c in range(col_groups):
                for s in range(strips):
                    member = (g * strips + s) ^ mask
                    source = (g * col_groups + c) * strips + s
                    target = ((member // strips) * col_groups + c) * strips + member % strips
                    pairs.append((source, target))
        return lax.ppermute(value, ("tile", "strip"), pairs)

    beyond = lax.ppermute(border(image), "strip", [(0, 1), (1, 0)])
    to_even, to_odd = edges(image, beyond)
    even_pairs = [(i, i ^ 1) for i in range(tiles)]
    odd_pairs = [(i, i + 1) for i in range(1, tiles - 1, 2)]
    odd_pairs = odd_pairs + [(j, i) for i, j in odd_pairs]
    odd = lax.ppermute(to_odd, "tile", odd_pairs)
    even = lax.ppermute(to_even, "tile", even_pairs)

    vectors_in = (row(bn_gain), row(bn_shift), row(b_expand), row(b_depth), row(b_project), w_depth)
    expanded, vectors = expand(image, w_expand, vectors_in)
    taps, outer = rim(rows, even, odd, beyond, w_expand, vectors)
    attend_weights = (row(attn_gain), row(attn_shift), w_qkv, w_out, table(rel_table))
    feed_weights = (row(ffn_gain), row(ffn_shift), w_up, row(b_up), w_down, row(b_down))
    heads = rel_table.shape[0]

    def after(first, then):
        return lax.optimization_barrier((first, then))

    def to_peer(outgoing, key):
        return exchange(outgoing[key], 4 * key[0] + 2 * key[1])

    far_keys = ((2, 0), (3, 0), (2, 1), (3, 1))
    near_keys = ((1, 0), (0, 1), (1, 1))

    def paired(own, from_core, first):
        return {
            (first + k, x): jnp.stack([own[k, x], from_core[k, x]]) for k in range(own.shape[0]) for x in range(2)
        }

    own, to_core = conv(0, expanded, image, taps, outer, w_project, vectors)
    outgoing = paired(own, exchange(to_core, 1), 0)
    arrived = {(0, 0): outgoing[0, 0]}
    arrived.update({key: to_peer(outgoing, key) for key in near_keys})
    own, to_core = conv(1, expanded, image, taps, outer, w_project, vectors)
    outgoing = paired(own, exchange(to_core, 1), 2)
    arrived.update({key: to_peer(outgoing, key) for key in far_keys})
    order = [(k, x) for k in range(4) for x in range(2)]
    own, to_core = attend([arrived[key] for key in order], heads, attend_weights)

    outgoing = paired(own, exchange(to_core, 1), 0)
    home = {(0, 0): outgoing[0, 0]}
    home.update({key: to_peer(outgoing, key) for key in near_keys})
    home[0, 1], outgoing = after(home[0, 1], outgoing)
    home.update({key: to_peer(outgoing, key) for key in far_keys})
    out = feed(0, [home[key] for key in order[:4]], feed_weights, image, None)
    return feed(1, [home[key] for key in order[4:]], feed_weights, image, out)


def solution(mesh):
    return jax.shard_map(
        local,
        mesh=mesh,
        in_specs=(P(("group", "strip"), "tile", None),) + (P(),) * 19,
        out_specs=P(("group", "strip"), "tile", None),
        check_vma=False,
    )
```

```python
import functools

import jax
import jax.numpy as jnp
from jax import lax
from jax.experimental import pallas as pl
from jax.experimental.pallas import tpu as pltpu
from jax.sharding import PartitionSpec as P

GRID = 8
EPSILON = 1e-05
F32 = jnp.float32
BF16 = jnp.bfloat16
SLAB = 8
ROW_GAIN, ROW_SHIFT, ROW_EXPAND, ROW_DEPTH, ROW_PROJECT, ROW_TAPS, ROWS = 0, 1, 2, 3, 4, 8, 24
LANES = 128
VMEM_LIMIT = 48 * 1024 * 1024


def dot(lhs, rhs):
    return jnp.dot(lhs, rhs, preferred_element_type=F32)


def dot_nt(lhs, rhs):
    return lax.dot_general(lhs, rhs, (((1,), (1,)), ((), ())), preferred_element_type=F32)


def gelu(v):
    half = 0.5 * v
    inner = v * (0.7978845608028654 + (0.7978845608028654 * 0.044715) * (v * v))
    return half + half * jnp.tanh(inner)


def layer_norm(x, gain, shift):
    center = jnp.mean(x, axis=-1, keepdims=True)
    diff = x - center
    spread = jnp.mean(diff * diff, axis=-1, keepdims=True)
    return diff * lax.rsqrt(spread + EPSILON) * gain + shift


def full(shape):
    return pl.BlockSpec(shape, lambda *_: (0,) * len(shape))


VMEM = pl.BlockSpec(memory_space=pltpu.VMEM)
ANY = pl.BlockSpec(memory_space=pl.ANY)
PARAMS = pltpu.CompilerParams(vmem_limit_bytes=VMEM_LIMIT)


class Place:
    def __init__(self):
        self.strips = lax.axis_size("strip")
        self.tiles = lax.axis_size("tile")
        self.col_groups = self.tiles // GRID
        self.strip = lax.axis_index("strip")
        self.tile = lax.axis_index("tile")
        grid_col = self.tile // self.col_groups
        self.zi = grid_col // 2
        self.xc = (grid_col % 2) * self.strips + self.strip
        self.odd = self.tile % 2


def split3(x):
    high = x.astype(BF16)
    rest = x - high.astype(F32)
    middle = rest.astype(BF16)
    return [high, middle, (rest - middle.astype(F32)).astype(BF16)]


def border_kernel(image_ref, out_ref):
    out_ref[...] = image_ref[jnp.where(Place().strip == 0, image_ref.shape[0] - 1, 0)]


def border(image):
    return pl.pallas_call(
        border_kernel,
        in_specs=[VMEM],
        out_specs=VMEM,
        out_shape=jax.ShapeDtypeStruct(image.shape[1:], BF16),
        compiler_params=PARAMS,
        name="border",
    )(image)


def edges_kernel(image_ref, beyond_ref, even_ref, odd_ref):
    place = Place()
    rows, cols, width = image_ref.shape
    pixels = image_ref[...].reshape(rows * cols, width)
    pick = lax.broadcasted_iota(jnp.int32, (2 * rows, rows * cols), 0)
    where = lax.broadcasted_iota(jnp.int32, (2 * rows, rows * cols), 1)
    first, last = place.odd, 1 - place.odd
    wanted = jnp.where(
        pick < rows, pick * cols + last * (cols - 1), (pick - rows) * cols + first * (cols - 1)
    )
    onehot = jnp.where(where == wanted, 1.0, 0.0).astype(BF16)
    columns = dot(onehot, pixels)
    beyond = beyond_ref[...].astype(F32)
    corners = [jnp.broadcast_to(beyond[c : c + 1], (2 * SLAB, width)) for c in (0, cols - 1)]
    for side, ref in ((0, even_ref), (1, odd_ref)):
        outer = place.odd == side
        corner = jnp.where(outer, corners[1], corners[0])
        ref[...] = jnp.concatenate([columns[side * rows : (side + 1) * rows], corner], axis=0).astype(BF16)


def edges(image, beyond):
    rows, cols, width = image.shape
    return pl.pallas_call(
        edges_kernel,
        out_shape=[jax.ShapeDtypeStruct((rows + 2 * SLAB, width), BF16)] * 2,
        compiler_params=PARAMS,
        cost_estimate=pl.CostEstimate(flops=4_000_000_000, bytes_accessed=1_000_000, transcendentals=0),
        name="edges",
    )(image, beyond)


def table_kernel(rel_ref, out_ref, rel_pad_ref, flat_ref):
    heads, entries = rel_ref.shape
    span = 2 * GRID - 1
    depth = rel_pad_ref.shape[1]
    rel_pad_ref[...] = jnp.zeros_like(rel_pad_ref)
    rel_pad_ref[:, :entries] = rel_ref[...]
    parts = jnp.concatenate(split3(rel_pad_ref[...]), axis=0)
    entry = lax.broadcasted_iota(jnp.int32, (depth, LANES), 0)
    lane = lax.broadcasted_iota(jnp.int32, (depth, LANES), 1)
    wanted = (lane % GRID + GRID - 1) * span + lane // GRID
    for k in range(GRID):
        onehot = jnp.where(entry == wanted - k * span, 1.0, 0.0).astype(BF16)
        found = dot(parts, onehot)
        flat_ref[k * heads : (k + 1) * heads, :] = (
            found[:heads] + found[heads : 2 * heads] + found[2 * heads :]
        )
    for h in range(heads):
        out_ref[h] = flat_ref[pl.ds(h, GRID, stride=heads), :]


def table(rel_table):
    heads, entries = rel_table.shape
    depth = -(-entries // LANES) * LANES
    return pl.pallas_call(
        table_kernel,
        out_shape=jax.ShapeDtypeStruct((heads, GRID, LANES), F32),
        scratch_shapes=[pltpu.VMEM((heads, depth), F32), pltpu.VMEM((GRID * heads, LANES), F32)],
        compiler_params=PARAMS,
        name="table",
    )(rel_table)


def expand_block(pixels, gain, shift, w_ref, bias, store):
    normed = (pixels.astype(F32) * gain + shift).astype(BF16)
    step = 2 * LANES
    for n in range(w_ref.shape[1] // step):
        part = slice(n * step, (n + 1) * step)
        store(part, gelu(dot(normed, w_ref[:, part]) + bias[:, part]))


def expand_kernel(image_ref, w_ref, *refs):
    out_ref, vectors_ref = refs[-2:]
    width, hidden = w_ref.shape
    vectors_ref[...] = jnp.zeros_like(vectors_ref)
    for line, ref in zip((ROW_GAIN, ROW_SHIFT, ROW_EXPAND, ROW_DEPTH, ROW_PROJECT, ROW_TAPS), refs):
        vectors_ref[line : line + ref.shape[0], : ref.shape[1]] = ref[...]
    rows, cols, _ = image_ref.shape
    gain = vectors_ref[ROW_GAIN : ROW_GAIN + 1, :width]
    shift = vectors_ref[ROW_SHIFT : ROW_SHIFT + 1, :width]

    def store(part, value):
        out_ref[:, :, part] = value.astype(BF16).reshape(rows, cols, value.shape[-1])

    pixels = image_ref[...].reshape(rows * cols, width)
    expand_block(pixels, gain, shift, w_ref, vectors_ref[ROW_EXPAND : ROW_EXPAND + 1, :], store)


def expand(image, w_expand, vectors):
    rows, cols, width = image.shape
    hidden = w_expand.shape[1]
    return pl.pallas_call(
        expand_kernel,
        in_specs=[VMEM] * (2 + len(vectors)),
        out_specs=[VMEM] * 2,
        out_shape=[
            jax.ShapeDtypeStruct((rows, cols, hidden), BF16),
            jax.ShapeDtypeStruct((ROWS, hidden), F32),
        ],
        compiler_params=PARAMS,
        cost_estimate=pl.CostEstimate(
            flops=16 * rows * cols * width * hidden, bytes_accessed=4_000_000, transcendentals=rows * cols * hidden
        ),
        name="expand",
    )(image, w_expand, *vectors)


def rim_kernel(even_ref, odd_ref, outer_ref, w_expand_ref, vectors_ref, tap_ref, beyond_ref, rim_ref, side_ref):
    place = Place()
    cols, width = outer_ref.shape
    rows = tap_ref.shape[1]

    def tap(t):
        return vectors_ref[ROW_TAPS + t : ROW_TAPS + t + 1, :]

    is_odd = place.odd == 1
    even, odd = even_ref[...].astype(F32), odd_ref[...].astype(F32)
    left, right = jnp.where(is_odd, even, odd), jnp.where(is_odd, odd, even)
    rim_in = jnp.concatenate([left, right, outer_ref[...].astype(F32)], axis=0)

    def store(part, value):
        rim_ref[:, part] = value.astype(BF16).astype(F32)

    expand_block(
        rim_in,
        vectors_ref[ROW_GAIN : ROW_GAIN + 1, :width],
        vectors_ref[ROW_SHIFT : ROW_SHIFT + 1, :width],
        w_expand_ref,
        vectors_ref[ROW_EXPAND : ROW_EXPAND + 1, :],
        store,
    )
    ok_up, ok_down = place.strip > 0, place.strip < place.strips - 1
    tall = rows + 2 * SLAB
    beyond_ref[...] = rim_ref[2 * tall : 2 * tall + cols, :].astype(BF16)
    for side, ok in ((0, place.tile > 0), (1, place.tile < place.tiles - 1)):
        base = side * tall
        corner = rim_ref[base + rows : base + rows + 1, :]
        side_ref[1 : rows + 1, :] = jnp.where(ok, rim_ref[base : base + rows, :], 0.0)
        side_ref[0:1, :] = jnp.where(jnp.logical_and(ok, ok_up), corner, 0.0)
        side_ref[rows + 1 : rows + 2, :] = jnp.where(jnp.logical_and(ok, ok_down), corner, 0.0)
        j = 2 * side
        tap_ref[side] = (
            side_ref[0:rows, :] * tap(j)
            + side_ref[1 : rows + 1, :] * tap(3 + j)
            + side_ref[2 : rows + 2, :] * tap(6 + j)
        )


def rim(rows, even, odd, outer, w_expand, vectors):
    hidden = w_expand.shape[1]
    cols = outer.shape[0]
    return pl.pallas_call(
        rim_kernel,
        in_specs=[VMEM] * 5,
        out_specs=[VMEM] * 2,
        out_shape=[
            jax.ShapeDtypeStruct((2, rows, hidden), F32),
            jax.ShapeDtypeStruct((cols, hidden), BF16),
        ],
        scratch_shapes=[
            pltpu.VMEM((2 * even.shape[0] + cols, hidden), F32),
            pltpu.VMEM((rows + SLAB, hidden), F32),
        ],
        compiler_params=PARAMS,
        cost_estimate=pl.CostEstimate(
            flops=2 * 4 * cols * outer.shape[1] * hidden, bytes_accessed=1_000_000, transcendentals=4 * cols * hidden
        ),
        name="rim",
    )(even, odd, outer, w_expand, vectors)


def conv_kernel(expanded_ref, image_ref, tap_ref, outer_ref, w_project_ref, vectors_ref, *refs):
    out_refs = (refs[2:4], refs[:2])
    section_ref, deep_ref = refs[4:]
    place = Place()
    rows, cols, width = image_ref.shape
    hidden = expanded_ref.shape[-1]
    groups = rows // SLAB
    octets = cols // SLAB
    half = SLAB // 2
    zi, xc = place.zi, place.xc
    ok_up, ok_down = place.strip > 0, place.strip < place.strips - 1
    slab_id = lax.broadcasted_iota(jnp.int32, (SLAB, LANES), 0)

    def chunk(index, carry):
        lanes = pl.ds(pl.multiple_of(index * LANES, LANES), LANES)
        weights = [vectors_ref[ROW_TAPS + t : ROW_TAPS + t + 1, lanes] for t in range(9)]
        bias = vectors_ref[ROW_DEPTH : ROW_DEPTH + 1, lanes]
        for m in range(groups):
            for p in range(2):
                start = m * SLAB + p * half
                lines = []
                for r in range(start - 1, start + half + 1):
                    if r < 0:
                        lines.append(jnp.where(ok_up, outer_ref[:, lanes].astype(F32), 0.0))
                    elif r >= rows:
                        lines.append(jnp.where(ok_down, outer_ref[:, lanes].astype(F32), 0.0))
                    else:
                        lines.append(expanded_ref[r, :, lanes].astype(F32))
                for q in range(half):
                    r = start + q
                    sums = [
                        lines[q] * weights[j] + lines[q + 1] * weights[3 + j] + lines[q + 2] * weights[6 + j]
                        for j in range(3)
                    ]
                    before, after = pltpu.roll(sums[0], 1, 0), pltpu.roll(sums[2], cols - 1, 0)
                    head = jnp.where(slab_id == 0, tap_ref[0, r : r + 1, lanes], before[:SLAB])
                    tail = jnp.where(slab_id == SLAB - 1, tap_ref[1, r : r + 1, lanes], after[-SLAB:])
                    before = jnp.concatenate([head, before[SLAB:]], axis=0)
                    after = jnp.concatenate([after[:-SLAB], tail], axis=0)
                    deep_ref[p, q, m, :, lanes] = gelu(before + sums[1] + after + bias).astype(BF16)
        return carry

    lax.fori_loop(0, hidden // LANES, chunk, 0)

    b_project = vectors_ref[ROW_PROJECT : ROW_PROJECT + 1, :width]
    for k in range(4):
        q = jnp.bitwise_xor(zi, k)
        for p in range(2):
            projected = dot(deep_ref[p, q].reshape(groups * cols, hidden), w_project_ref[...]) + b_project
            own = jnp.stack([image_ref[m * SLAB + p * half + q] for m in range(groups)]).astype(F32)
            section = (own + projected.reshape(groups, cols, width)).reshape(groups, octets, SLAB, width)
            for o in range(octets):
                section_ref[k, p, o] = section[:, o].reshape(groups * SLAB, width)
            for j in range(4):
                out_refs[k // 2][j % 2][k % 2, j // 2, p] = section_ref[k, p, jnp.bitwise_xor(xc, j)].astype(BF16)


def conv(expanded, image, taps, outer, w_project, vectors):
    rows, cols, width = image.shape
    hidden = expanded.shape[-1]
    groups = rows // SLAB
    octets = cols // SLAB
    shape = jax.ShapeDtypeStruct((2, 2, 2, groups * SLAB, width), BF16)
    return pl.pallas_call(
        conv_kernel,
        in_specs=[VMEM] * 6,
        out_specs=[VMEM] * 4,
        out_shape=[shape] * 4,
        scratch_shapes=[
            pltpu.VMEM((4, 2, octets, groups * SLAB, width), F32),
            pltpu.VMEM((2, 4, groups, cols, hidden), BF16),
        ],
        compiler_params=PARAMS,
        cost_estimate=pl.CostEstimate(
            flops=2 * rows * cols * width * hidden, bytes_accessed=6_000_000, transcendentals=rows * cols * hidden
        ),
        name="conv",
    )(expanded, image, taps, outer, w_project, vectors)


def attend_kernel(heads, *refs):
    in_refs, refs = refs[:8], refs[8:]
    gain_ref, shift_ref, w_qkv_ref, w_out_ref, table_ref = refs[:5]
    out_refs = (refs[7:9], refs[5:7])
    token_ref, normed_ref, query_t_ref, value_t_ref, bias_ref, window_ref, key_ref, qt_ref, vt_ref, context_ref = refs[9:]
    place = Place()
    zi, xc = place.zi, place.xc
    halves, count, _ = normed_ref.shape
    width = halves * LANES
    chunk_rows = token_ref.shape[2]
    head = width // heads
    tokens = GRID * GRID
    wins = chunk_rows // 4
    sources = tokens // 4

    def spot_of(p, slot):
        return pl.ds(pl.multiple_of((p * sources + slot) * chunk_rows, chunk_rows), chunk_rows)

    def slot_of(k, j):
        return jnp.bitwise_xor(zi, k) * 4 + jnp.bitwise_xor(xc, j)

    for k in range(4):
        for j in range(4):
            slot = slot_of(k, j)
            for p in range(2):
                x = in_refs[2 * k + j // 2][j % 2, p].astype(F32)
                token_ref[p, slot] = x
                normed = layer_norm(x, gain_ref[...], shift_ref[...])
                for c in range(halves):
                    normed_ref[c, spot_of(p, slot), :] = normed[:, c * LANES : (c + 1) * LANES]

    query_t_ref[...] = w_qkv_ref[:, :width].T
    value_t_ref[...] = w_qkv_ref[:, 2 * width :].T
    left_half = lax.broadcasted_iota(jnp.int32, (tokens, 2 * tokens), 1) < tokens
    row_head = lax.broadcasted_iota(jnp.int32, (LANES, 2 * tokens), 0) // head
    per_group = LANES // head

    lane_half = lax.broadcasted_iota(jnp.int32, (GRID, 2 * tokens), 1) < tokens
    for h in range(heads):
        base = table_ref[h]
        for c in range(GRID):
            off = (GRID - 1 - c) * GRID
            one = pltpu.roll(base, (LANES - off) % LANES, 1)
            two = pltpu.roll(base, (LANES - off + tokens) % LANES, 1)
            bias_ref[h, c * GRID : (c + 1) * GRID, :] = jnp.where(lane_half, one, two)

    def window(win):
        return pl.ds((win // wins) * tokens * wins + win % wins, tokens, stride=wins)

    for win in range(2 * wins):
        picked = [normed_ref[c, window(win), :] for c in range(halves)]
        window_ref[win * tokens : (win + 1) * tokens, :] = jnp.concatenate(picked, axis=1).astype(BF16)
    normed = window_ref[...]
    key_ref[...] = dot(normed, w_qkv_ref[:, width : 2 * width]).astype(BF16)
    qt_ref[...] = (dot_nt(query_t_ref[...], normed) * head ** (-0.5)).astype(BF16)
    vt_ref[...] = dot_nt(value_t_ref[...], normed).astype(BF16)

    for pair in range(wins):
        lanes = slice(pair * 2 * tokens, (pair + 1) * 2 * tokens)
        for h in range(heads):
            g = h // per_group
            span = slice(g * LANES, (g + 1) * LANES)
            own = jnp.where(row_head == h % per_group, qt_ref[span, lanes], jnp.zeros((), BF16))
            both = dot(key_ref[lanes, span], own)
            scores = jnp.where(left_half, both[:tokens], both[tokens:]) + bias_ref[h]
            weight = jnp.exp(scores - jnp.max(scores, axis=0, keepdims=True))
            probs = weight * (1.0 / jnp.sum(weight, axis=0, keepdims=True))
            spread = jnp.concatenate(
                [jnp.where(left_half, probs, 0.0), jnp.where(left_half, 0.0, probs)], axis=0
            ).astype(BF16)
            context_ref[h * head : (h + 1) * head, lanes] = dot(vt_ref[h * head : (h + 1) * head, lanes], spread)
    context = context_ref[...].T.astype(BF16)
    attended = dot(context, w_out_ref[...])
    for win in range(2 * wins):
        for c in range(halves):
            normed_ref[c, window(win), :] = attended[
                win * tokens : (win + 1) * tokens, c * LANES : (c + 1) * LANES
            ]

    for k in range(4):
        for j in range(4):
            slot = slot_of(k, j)
            ref = out_refs[k // 2][j % 2]
            for p in range(2):
                added = jnp.concatenate([normed_ref[c, spot_of(p, slot), :] for c in range(halves)], axis=1)
                ref[k % 2, j // 2, p] = (token_ref[p, slot] + added).astype(BF16)


def attend(arrived, heads, weights):
    chunk_rows, width = arrived[0].shape[2:]
    count = 32 * chunk_rows
    flops = 2 * count * width * (4 * width)
    tokens = GRID * GRID
    shape = jax.ShapeDtypeStruct((2, 2, 2, chunk_rows, width), BF16)
    return pl.pallas_call(
        functools.partial(attend_kernel, heads),
        in_specs=[VMEM] * 13,
        out_specs=[VMEM] * 4,
        out_shape=[shape] * 4,
        scratch_shapes=[
            pltpu.VMEM((2, 16, chunk_rows, width), F32),
            pltpu.VMEM((width // LANES, count, LANES), F32),
            pltpu.VMEM((width, width), BF16),
            pltpu.VMEM((width, width), BF16),
            pltpu.VMEM((heads, tokens, 2 * tokens), F32),
            pltpu.VMEM((count, width), BF16),
            pltpu.VMEM((count, width), BF16),
            pltpu.VMEM((width, count), BF16),
            pltpu.VMEM((width, count), BF16),
            pltpu.VMEM((width, count), F32),
        ],
        compiler_params=PARAMS,
        cost_estimate=pl.CostEstimate(flops=flops, bytes_accessed=4_000_000, transcendentals=count * 512),
        name="attend",
    )(*arrived, *weights)


def feed_kernel(places, *refs):
    parts = 2 * len(places)
    in_refs, refs = refs[:parts], refs[parts:]
    gain_ref, shift_ref, w_up_ref, b_up_ref, w_down_ref, b_down_ref = refs[:6]
    out_ref, line_ref, section_ref, sems = refs[-4:]
    place = Place()
    zi, xc = place.zi, place.xc
    _, _, groups, cols, width = line_ref.shape
    half = SLAB // 2
    step = 2 * LANES
    copies = []
    for n, k in enumerate(places):
        for p in range(2):
            for j in range(4):
                o = jnp.bitwise_xor(xc, j)
                section_ref[n, p, o] = in_refs[2 * n + j // 2][j % 2, p].astype(F32)
            slabs = [section_ref[n, p, o].reshape(groups, 1, SLAB, width) for o in range(cols // SLAB)]
            section = jnp.concatenate(slabs, axis=1).reshape(groups * cols, width)
            normed = layer_norm(section, gain_ref[...], shift_ref[...]).astype(BF16)
            total = section + b_down_ref[...]
            for i in range(w_up_ref.shape[1] // step):
                inner = slice(i * step, (i + 1) * step)
                hidden = gelu(dot(normed, w_up_ref[:, inner]) + b_up_ref[:, inner]).astype(BF16)
                total = total + dot(hidden, w_down_ref[inner, :])
            line_ref[n, p] = total.reshape(groups, cols, width).astype(BF16)
            for m in range(groups):
                r = m * SLAB + p * half + jnp.bitwise_xor(zi, k)
                copies.append(
                    pltpu.make_async_copy(line_ref.at[n, p, m], out_ref.at[r], sems.at[len(copies)])
                )
    for copy in copies:
        copy.start()
    for copy in copies:
        copy.wait()


def feed(places, sections, weights, image, partial):
    rows, cols, width = image.shape
    groups = rows // SLAB
    hidden = weights[2].shape[1]
    held = len(sections) + len(weights)
    count = len(places) * rows * cols // 4
    extra = [] if partial is None else [partial]
    return pl.pallas_call(
        functools.partial(feed_kernel, places),
        in_specs=[VMEM] * held + [ANY] * len(extra),
        out_specs=ANY,
        out_shape=jax.ShapeDtypeStruct(image.shape, BF16),
        scratch_shapes=[
            pltpu.VMEM((len(places), 2, groups, cols, width), BF16),
            pltpu.VMEM((len(places), 2, cols // SLAB, groups * SLAB, width), F32),
            pltpu.SemaphoreType.DMA((2 * len(places) * groups,)),
        ],
        input_output_aliases={held: 0} if extra else {},
        compiler_params=PARAMS,
        cost_estimate=pl.CostEstimate(
            flops=4 * count * width * hidden, bytes_accessed=2_000_000, transcendentals=count * hidden
        ),
        name="feed",
    )(*sections, *weights, *extra)


def local(
    image,
    bn_gain,
    bn_shift,
    w_expand,
    b_expand,
    w_depth,
    b_depth,
    w_project,
    b_project,
    attn_gain,
    attn_shift,
    w_qkv,
    w_out,
    rel_table,
    ffn_gain,
    ffn_shift,
    w_up,
    b_up,
    w_down,
    b_down,
):
    rows, cols, width = image.shape
    strips = lax.axis_size("strip")
    tiles = lax.axis_size("tile")
    col_groups = tiles // GRID
    assert strips == 2 and rows * strips == GRID * SLAB and cols == 4 * SLAB

    def row(v):
        return v.reshape(1, -1)

    def exchange(value, mask):
        pairs = []
        for g in range(GRID):
            for c in range(col_groups):
                for s in range(strips):
                    member = (g * strips + s) ^ mask
                    source = (g * col_groups + c) * strips + s
                    target = ((member // strips) * col_groups + c) * strips + member % strips
                    pairs.append((source, target))
        return lax.ppermute(value, ("tile", "strip"), pairs)

    beyond = lax.ppermute(border(image), "strip", [(0, 1), (1, 0)])
    to_even, to_odd = edges(image, beyond)
    even_pairs = [(i, i ^ 1) for i in range(tiles)]
    odd_pairs = [(i, i + 1) for i in range(1, tiles - 1, 2)]
    odd_pairs = odd_pairs + [(j, i) for i, j in odd_pairs]
    odd = lax.ppermute(to_odd, "tile", odd_pairs)
    even = lax.ppermute(to_even, "tile", even_pairs)

    vectors_in = (row(bn_gain), row(bn_shift), row(b_expand), row(b_depth), row(b_project), w_depth)
    expanded, vectors = expand(image, w_expand, vectors_in)
    taps, outer = rim(rows, even, odd, beyond, w_expand, vectors)
    attend_weights = (row(attn_gain), row(attn_shift), w_qkv, w_out, table(rel_table))
    feed_weights = (row(ffn_gain), row(ffn_shift), w_up, row(b_up), w_down, row(b_down))
    heads = rel_table.shape[0]

    def after(first, then):
        return lax.optimization_barrier((first, then))

    def to_peer(outgoing, key):
        return exchange(outgoing[key], 4 * key[0] + 2 * key[1])

    far_keys = ((2, 0), (3, 0), (2, 1), (3, 1))
    near_keys = ((1, 0), (0, 1), (1, 1))

    def paired(own, from_core, first):
        return {
            (first + k, x): jnp.stack([own[k, x], from_core[k, x]]) for k in range(own.shape[0]) for x in range(2)
        }

    def spread(own_f, to_core_f, own_n, to_core_n):
        outgoing = paired(own_f, exchange(to_core_f, 1), 2)
        arrived = {key: to_peer(outgoing, key) for key in far_keys}
        outgoing = paired(own_n, exchange(to_core_n, 1), 0)
        arrived[0, 0] = outgoing[0, 0]
        arrived.update({key: to_peer(outgoing, key) for key in near_keys})
        return [arrived[k, x] for k in range(4) for x in range(2)]

    held = spread(*conv(expanded, image, taps, outer, w_project, vectors))
    home = spread(*attend(held, heads, attend_weights))
    return feed((0, 1, 2, 3), home, feed_weights, image, None)


def solution(mesh):
    return jax.shard_map(
        local,
        mesh=mesh,
        in_specs=(P(("group", "strip"), "tile", None),) + (P(),) * 19,
        out_specs=P(("group", "strip"), "tile", None),
        check_vma=False,
    )
```

```python
import functools

import jax
import jax.numpy as jnp
from jax import lax
from jax.experimental import pallas as pl
from jax.experimental.pallas import tpu as pltpu
from jax.sharding import PartitionSpec as P

GRID = 8
EPSILON = 1e-05
F32 = jnp.float32
BF16 = jnp.bfloat16
SLAB = 8
ROW_GAIN, ROW_SHIFT, ROW_EXPAND, ROW_DEPTH, ROW_PROJECT, ROW_TAPS, ROWS = 0, 1, 2, 3, 4, 8, 24
LANES = 128
VMEM_LIMIT = 48 * 1024 * 1024


def dot(lhs, rhs):
    return jnp.dot(lhs, rhs, preferred_element_type=F32)


def dot_nt(lhs, rhs):
    return lax.dot_general(lhs, rhs, (((1,), (1,)), ((), ())), preferred_element_type=F32)


def gelu(v):
    half = 0.5 * v
    inner = v * (0.7978845608028654 + (0.7978845608028654 * 0.044715) * (v * v))
    return half + half * jnp.tanh(inner)


def layer_norm(x, gain, shift):
    center = jnp.mean(x, axis=-1, keepdims=True)
    diff = x - center
    spread = jnp.mean(diff * diff, axis=-1, keepdims=True)
    return diff * lax.rsqrt(spread + EPSILON) * gain + shift


def full(shape):
    return pl.BlockSpec(shape, lambda *_: (0,) * len(shape))


VMEM = pl.BlockSpec(memory_space=pltpu.VMEM)
ANY = pl.BlockSpec(memory_space=pl.ANY)
PARAMS = pltpu.CompilerParams(vmem_limit_bytes=VMEM_LIMIT)


class Place:
    def __init__(self):
        self.strips = lax.axis_size("strip")
        self.tiles = lax.axis_size("tile")
        self.col_groups = self.tiles // GRID
        self.strip = lax.axis_index("strip")
        self.tile = lax.axis_index("tile")
        grid_col = self.tile // self.col_groups
        self.zi = grid_col // 2
        self.xc = (grid_col % 2) * self.strips + self.strip
        self.odd = self.tile % 2


def split3(x):
    high = x.astype(BF16)
    rest = x - high.astype(F32)
    middle = rest.astype(BF16)
    return [high, middle, (rest - middle.astype(F32)).astype(BF16)]


def border_kernel(image_ref, out_ref):
    out_ref[...] = image_ref[jnp.where(Place().strip == 0, image_ref.shape[0] - 1, 0)]


def border(image):
    return pl.pallas_call(
        border_kernel,
        in_specs=[VMEM],
        out_specs=VMEM,
        out_shape=jax.ShapeDtypeStruct(image.shape[1:], BF16),
        compiler_params=PARAMS,
        name="border",
    )(image)


def edges_kernel(image_ref, beyond_ref, even_ref, odd_ref):
    place = Place()
    rows, cols, width = image_ref.shape
    pixels = image_ref[...].reshape(rows * cols, width)
    pick = lax.broadcasted_iota(jnp.int32, (2 * rows, rows * cols), 0)
    where = lax.broadcasted_iota(jnp.int32, (2 * rows, rows * cols), 1)
    first, last = place.odd, 1 - place.odd
    wanted = jnp.where(
        pick < rows, pick * cols + last * (cols - 1), (pick - rows) * cols + first * (cols - 1)
    )
    onehot = jnp.where(where == wanted, 1.0, 0.0).astype(BF16)
    columns = dot(onehot, pixels)
    beyond = beyond_ref[...].astype(F32)
    corners = [jnp.broadcast_to(beyond[c : c + 1], (2 * SLAB, width)) for c in (0, cols - 1)]
    for side, ref in ((0, even_ref), (1, odd_ref)):
        outer = place.odd == side
        corner = jnp.where(outer, corners[1], corners[0])
        ref[...] = jnp.concatenate([columns[side * rows : (side + 1) * rows], corner], axis=0).astype(BF16)


def edges(image, beyond):
    rows, cols, width = image.shape
    return pl.pallas_call(
        edges_kernel,
        out_shape=[jax.ShapeDtypeStruct((rows + 2 * SLAB, width), BF16)] * 2,
        compiler_params=PARAMS,
        cost_estimate=pl.CostEstimate(flops=4_000_000_000, bytes_accessed=1_000_000, transcendentals=0),
        name="edges",
    )(image, beyond)


def table_kernel(rel_ref, out_ref, rel_pad_ref, flat_ref):
    heads, entries = rel_ref.shape
    span = 2 * GRID - 1
    depth = rel_pad_ref.shape[1]
    rel_pad_ref[...] = jnp.zeros_like(rel_pad_ref)
    rel_pad_ref[:, :entries] = rel_ref[...]
    parts = jnp.concatenate(split3(rel_pad_ref[...]), axis=0)
    entry = lax.broadcasted_iota(jnp.int32, (depth, LANES), 0)
    lane = lax.broadcasted_iota(jnp.int32, (depth, LANES), 1)
    wanted = (lane % GRID + GRID - 1) * span + lane // GRID
    for k in range(GRID):
        onehot = jnp.where(entry == wanted - k * span, 1.0, 0.0).astype(BF16)
        found = dot(parts, onehot)
        flat_ref[k * heads : (k + 1) * heads, :] = (
            found[:heads] + found[heads : 2 * heads] + found[2 * heads :]
        )
    for h in range(heads):
        out_ref[h] = flat_ref[pl.ds(h, GRID, stride=heads), :]


def table(rel_table):
    heads, entries = rel_table.shape
    depth = -(-entries // LANES) * LANES
    return pl.pallas_call(
        table_kernel,
        out_shape=jax.ShapeDtypeStruct((heads, GRID, LANES), F32),
        scratch_shapes=[pltpu.VMEM((heads, depth), F32), pltpu.VMEM((GRID * heads, LANES), F32)],
        compiler_params=PARAMS,
        name="table",
    )(rel_table)


def expand_block(pixels, gain, shift, w_ref, bias, store):
    normed = (pixels.astype(F32) * gain + shift).astype(BF16)
    step = 2 * LANES
    for n in range(w_ref.shape[1] // step):
        part = slice(n * step, (n + 1) * step)
        store(part, gelu(dot(normed, w_ref[:, part]) + bias[:, part]))


def expand_kernel(image_ref, w_ref, *refs):
    out_ref, vectors_ref = refs[-2:]
    width, hidden = w_ref.shape
    vectors_ref[...] = jnp.zeros_like(vectors_ref)
    for line, ref in zip((ROW_GAIN, ROW_SHIFT, ROW_EXPAND, ROW_DEPTH, ROW_PROJECT, ROW_TAPS), refs):
        vectors_ref[line : line + ref.shape[0], : ref.shape[1]] = ref[...]
    rows, cols, _ = image_ref.shape
    gain = vectors_ref[ROW_GAIN : ROW_GAIN + 1, :width]
    shift = vectors_ref[ROW_SHIFT : ROW_SHIFT + 1, :width]

    def store(part, value):
        out_ref[:, :, part] = value.astype(BF16).reshape(rows, cols, value.shape[-1])

    pixels = image_ref[...].reshape(rows * cols, width)
    expand_block(pixels, gain, shift, w_ref, vectors_ref[ROW_EXPAND : ROW_EXPAND + 1, :], store)


def expand(image, w_expand, vectors):
    rows, cols, width = image.shape
    hidden = w_expand.shape[1]
    return pl.pallas_call(
        expand_kernel,
        in_specs=[VMEM] * (2 + len(vectors)),
        out_specs=[VMEM] * 2,
        out_shape=[
            jax.ShapeDtypeStruct((rows, cols, hidden), BF16),
            jax.ShapeDtypeStruct((ROWS, hidden), F32),
        ],
        compiler_params=PARAMS,
        cost_estimate=pl.CostEstimate(
            flops=16 * rows * cols * width * hidden, bytes_accessed=4_000_000, transcendentals=rows * cols * hidden
        ),
        name="expand",
    )(image, w_expand, *vectors)


def rim_kernel(even_ref, odd_ref, outer_ref, w_expand_ref, vectors_ref, tap_ref, beyond_ref, rim_ref, side_ref):
    place = Place()
    cols, width = outer_ref.shape
    rows = tap_ref.shape[1]

    def tap(t):
        return vectors_ref[ROW_TAPS + t : ROW_TAPS + t + 1, :]

    is_odd = place.odd == 1
    even, odd = even_ref[...].astype(F32), odd_ref[...].astype(F32)
    left, right = jnp.where(is_odd, even, odd), jnp.where(is_odd, odd, even)
    rim_in = jnp.concatenate([left, right, outer_ref[...].astype(F32)], axis=0)

    def store(part, value):
        rim_ref[:, part] = value.astype(BF16).astype(F32)

    expand_block(
        rim_in,
        vectors_ref[ROW_GAIN : ROW_GAIN + 1, :width],
        vectors_ref[ROW_SHIFT : ROW_SHIFT + 1, :width],
        w_expand_ref,
        vectors_ref[ROW_EXPAND : ROW_EXPAND + 1, :],
        store,
    )
    ok_up, ok_down = place.strip > 0, place.strip < place.strips - 1
    tall = rows + 2 * SLAB
    beyond_ref[...] = rim_ref[2 * tall : 2 * tall + cols, :].astype(BF16)
    for side, ok in ((0, place.tile > 0), (1, place.tile < place.tiles - 1)):
        base = side * tall
        corner = rim_ref[base + rows : base + rows + 1, :]
        side_ref[1 : rows + 1, :] = jnp.where(ok, rim_ref[base : base + rows, :], 0.0)
        side_ref[0:1, :] = jnp.where(jnp.logical_and(ok, ok_up), corner, 0.0)
        side_ref[rows + 1 : rows + 2, :] = jnp.where(jnp.logical_and(ok, ok_down), corner, 0.0)
        j = 2 * side
        tap_ref[side] = (
            side_ref[0:rows, :] * tap(j)
            + side_ref[1 : rows + 1, :] * tap(3 + j)
            + side_ref[2 : rows + 2, :] * tap(6 + j)
        )


def rim(rows, even, odd, outer, w_expand, vectors):
    hidden = w_expand.shape[1]
    cols = outer.shape[0]
    return pl.pallas_call(
        rim_kernel,
        in_specs=[VMEM] * 5,
        out_specs=[VMEM] * 2,
        out_shape=[
            jax.ShapeDtypeStruct((2, rows, hidden), F32),
            jax.ShapeDtypeStruct((cols, hidden), BF16),
        ],
        scratch_shapes=[
            pltpu.VMEM((2 * even.shape[0] + cols, hidden), F32),
            pltpu.VMEM((rows + SLAB, hidden), F32),
        ],
        compiler_params=PARAMS,
        cost_estimate=pl.CostEstimate(
            flops=2 * 4 * cols * outer.shape[1] * hidden, bytes_accessed=1_000_000, transcendentals=4 * cols * hidden
        ),
        name="rim",
    )(even, odd, outer, w_expand, vectors)


def conv_kernel(expanded_ref, image_ref, tap_ref, outer_ref, w_project_ref, vectors_ref, *refs):
    out_refs = (refs[2:4], refs[:2])
    section_ref, deep_ref = refs[4:]
    place = Place()
    rows, cols, width = image_ref.shape
    hidden = expanded_ref.shape[-1]
    groups = rows // SLAB
    octets = cols // SLAB
    half = SLAB // 2
    zi, xc = place.zi, place.xc
    ok_up, ok_down = place.strip > 0, place.strip < place.strips - 1
    slab_id = lax.broadcasted_iota(jnp.int32, (SLAB, LANES), 0)

    def chunk(index, carry):
        lanes = pl.ds(pl.multiple_of(index * LANES, LANES), LANES)
        weights = [vectors_ref[ROW_TAPS + t : ROW_TAPS + t + 1, lanes] for t in range(9)]
        bias = vectors_ref[ROW_DEPTH : ROW_DEPTH + 1, lanes]
        for m in range(groups):
            for p in range(2):
                start = m * SLAB + p * half
                lines = []
                for r in range(start - 1, start + half + 1):
                    if r < 0:
                        lines.append(jnp.where(ok_up, outer_ref[:, lanes].astype(F32), 0.0))
                    elif r >= rows:
                        lines.append(jnp.where(ok_down, outer_ref[:, lanes].astype(F32), 0.0))
                    else:
                        lines.append(expanded_ref[r, :, lanes].astype(F32))
                for q in range(half):
                    r = start + q
                    sums = [
                        lines[q] * weights[j] + lines[q + 1] * weights[3 + j] + lines[q + 2] * weights[6 + j]
                        for j in range(3)
                    ]
                    before, after = pltpu.roll(sums[0], 1, 0), pltpu.roll(sums[2], cols - 1, 0)
                    head = jnp.where(slab_id == 0, tap_ref[0, r : r + 1, lanes], before[:SLAB])
                    tail = jnp.where(slab_id == SLAB - 1, tap_ref[1, r : r + 1, lanes], after[-SLAB:])
                    before = jnp.concatenate([head, before[SLAB:]], axis=0)
                    after = jnp.concatenate([after[:-SLAB], tail], axis=0)
                    deep_ref[p, q, m, :, lanes] = gelu(before + sums[1] + after + bias).astype(BF16)
        return carry

    lax.fori_loop(0, hidden // LANES, chunk, 0)

    b_project = vectors_ref[ROW_PROJECT : ROW_PROJECT + 1, :width]
    for k in range(4):
        q = jnp.bitwise_xor(zi, k)
        for p in range(2):
            projected = dot(deep_ref[p, q].reshape(groups * cols, hidden), w_project_ref[...]) + b_project
            own = jnp.stack([image_ref[m * SLAB + p * half + q] for m in range(groups)]).astype(F32)
            section = (own + projected.reshape(groups, cols, width)).reshape(groups, octets, SLAB, width)
            for o in range(octets):
                section_ref[k, p, o] = section[:, o].reshape(groups * SLAB, width)
            for j in range(4):
                out_refs[k // 2][j % 2][k % 2, j // 2, p] = section_ref[k, p, jnp.bitwise_xor(xc, j)].astype(BF16)


def conv(expanded, image, taps, outer, w_project, vectors):
    rows, cols, width = image.shape
    hidden = expanded.shape[-1]
    groups = rows // SLAB
    octets = cols // SLAB
    shape = jax.ShapeDtypeStruct((2, 2, 2, groups * SLAB, width), BF16)
    return pl.pallas_call(
        conv_kernel,
        in_specs=[VMEM] * 6,
        out_specs=[VMEM] * 4,
        out_shape=[shape] * 4,
        scratch_shapes=[
            pltpu.VMEM((4, 2, octets, groups * SLAB, width), F32),
            pltpu.VMEM((2, 4, groups, cols, hidden), BF16),
        ],
        compiler_params=PARAMS,
        cost_estimate=pl.CostEstimate(
            flops=2 * rows * cols * width * hidden, bytes_accessed=6_000_000, transcendentals=rows * cols * hidden
        ),
        name="conv",
    )(expanded, image, taps, outer, w_project, vectors)


def attend_kernel(heads, *refs):
    in_refs, refs = refs[:8], refs[8:]
    gain_ref, shift_ref, w_qkv_ref, w_out_ref, table_ref = refs[:5]
    out_refs = (refs[7:9], refs[5:7])
    token_ref, normed_ref, query_t_ref, value_t_ref, bias_ref, window_ref, key_ref, qt_ref, vt_ref, context_ref = refs[9:]
    place = Place()
    zi, xc = place.zi, place.xc
    halves, count, _ = normed_ref.shape
    width = halves * LANES
    chunk_rows = token_ref.shape[2]
    head = width // heads
    tokens = GRID * GRID
    wins = chunk_rows // 4
    sources = tokens // 4

    def spot_of(p, slot):
        return pl.ds(pl.multiple_of((p * sources + slot) * chunk_rows, chunk_rows), chunk_rows)

    def slot_of(k, j):
        return jnp.bitwise_xor(zi, k) * 4 + jnp.bitwise_xor(xc, j)

    for k in range(4):
        for j in range(4):
            slot = slot_of(k, j)
            for p in range(2):
                x = in_refs[2 * k + j // 2][j % 2, p].astype(F32)
                token_ref[p, slot] = x
                normed = layer_norm(x, gain_ref[...], shift_ref[...])
                for c in range(halves):
                    normed_ref[c, spot_of(p, slot), :] = normed[:, c * LANES : (c + 1) * LANES]

    query_t_ref[...] = w_qkv_ref[:, :width].T
    value_t_ref[...] = w_qkv_ref[:, 2 * width :].T
    left_half = lax.broadcasted_iota(jnp.int32, (tokens, 2 * tokens), 1) < tokens
    row_head = lax.broadcasted_iota(jnp.int32, (LANES, 2 * tokens), 0) // head
    per_group = LANES // head

    lane_half = lax.broadcasted_iota(jnp.int32, (GRID, 2 * tokens), 1) < tokens
    for h in range(heads):
        base = table_ref[h]
        for c in range(GRID):
            off = (GRID - 1 - c) * GRID
            one = pltpu.roll(base, (LANES - off) % LANES, 1)
            two = pltpu.roll(base, (LANES - off + tokens) % LANES, 1)
            bias_ref[h, c * GRID : (c + 1) * GRID, :] = jnp.where(lane_half, one, two)

    def window(win):
        return pl.ds((win // wins) * tokens * wins + win % wins, tokens, stride=wins)

    for win in range(2 * wins):
        picked = [normed_ref[c, window(win), :] for c in range(halves)]
        window_ref[win * tokens : (win + 1) * tokens, :] = jnp.concatenate(picked, axis=1).astype(BF16)
    normed = window_ref[...]
    key_ref[...] = dot(normed, w_qkv_ref[:, width : 2 * width]).astype(BF16)
    qt_ref[...] = (dot_nt(query_t_ref[...], normed) * head ** (-0.5)).astype(BF16)
    vt_ref[...] = dot_nt(value_t_ref[...], normed).astype(BF16)

    for pair in range(wins):
        lanes = slice(pair * 2 * tokens, (pair + 1) * 2 * tokens)
        for h in range(heads):
            g = h // per_group
            span = slice(g * LANES, (g + 1) * LANES)
            own = jnp.where(row_head == h % per_group, qt_ref[span, lanes], jnp.zeros((), BF16))
            both = dot(key_ref[lanes, span], own)
            scores = jnp.where(left_half, both[:tokens], both[tokens:]) + bias_ref[h]
            weight = jnp.exp(scores - jnp.max(scores, axis=0, keepdims=True))
            probs = weight * (1.0 / jnp.sum(weight, axis=0, keepdims=True))
            spread = jnp.concatenate(
                [jnp.where(left_half, probs, 0.0), jnp.where(left_half, 0.0, probs)], axis=0
            ).astype(BF16)
            context_ref[h * head : (h + 1) * head, lanes] = dot(vt_ref[h * head : (h + 1) * head, lanes], spread)
    context = context_ref[...].T.astype(BF16)
    attended = dot(context, w_out_ref[...])
    for win in range(2 * wins):
        for c in range(halves):
            normed_ref[c, window(win), :] = attended[
                win * tokens : (win + 1) * tokens, c * LANES : (c + 1) * LANES
            ]

    for k in range(4):
        for j in range(4):
            slot = slot_of(k, j)
            ref = out_refs[k // 2][j % 2]
            for p in range(2):
                added = jnp.concatenate([normed_ref[c, spot_of(p, slot), :] for c in range(halves)], axis=1)
                ref[k % 2, j // 2, p] = (token_ref[p, slot] + added).astype(BF16)


def attend(arrived, heads, weights):
    chunk_rows, width = arrived[0].shape[2:]
    count = 32 * chunk_rows
    flops = 2 * count * width * (4 * width)
    tokens = GRID * GRID
    shape = jax.ShapeDtypeStruct((2, 2, 2, chunk_rows, width), BF16)
    return pl.pallas_call(
        functools.partial(attend_kernel, heads),
        in_specs=[VMEM] * 13,
        out_specs=[VMEM] * 4,
        out_shape=[shape] * 4,
        scratch_shapes=[
            pltpu.VMEM((2, 16, chunk_rows, width), F32),
            pltpu.VMEM((width // LANES, count, LANES), F32),
            pltpu.VMEM((width, width), BF16),
            pltpu.VMEM((width, width), BF16),
            pltpu.VMEM((heads, tokens, 2 * tokens), F32),
            pltpu.VMEM((count, width), BF16),
            pltpu.VMEM((count, width), BF16),
            pltpu.VMEM((width, count), BF16),
            pltpu.VMEM((width, count), BF16),
            pltpu.VMEM((width, count), F32),
        ],
        compiler_params=PARAMS,
        cost_estimate=pl.CostEstimate(flops=flops, bytes_accessed=4_000_000, transcendentals=count * 512),
        name="attend",
    )(*arrived, *weights)


def feed_kernel(places, *refs):
    parts = 2 * len(places)
    in_refs, refs = refs[:parts], refs[parts:]
    gain_ref, shift_ref, w_up_ref, b_up_ref, w_down_ref, b_down_ref = refs[:6]
    out_ref, line_ref, section_ref, sems = refs[-4:]
    place = Place()
    zi, xc = place.zi, place.xc
    _, _, groups, cols, width = line_ref.shape
    half = SLAB // 2
    step = 2 * LANES
    copies = []
    for n, k in enumerate(places):
        for p in range(2):
            for j in range(4):
                o = jnp.bitwise_xor(xc, j)
                section_ref[n, p, o] = in_refs[2 * n + j // 2][j % 2, p].astype(F32)
            slabs = [section_ref[n, p, o].reshape(groups, 1, SLAB, width) for o in range(cols // SLAB)]
            section = jnp.concatenate(slabs, axis=1).reshape(groups * cols, width)
            normed = layer_norm(section, gain_ref[...], shift_ref[...]).astype(BF16)
            total = section + b_down_ref[...]
            for i in range(w_up_ref.shape[1] // step):
                inner = slice(i * step, (i + 1) * step)
                hidden = gelu(dot(normed, w_up_ref[:, inner]) + b_up_ref[:, inner]).astype(BF16)
                total = total + dot(hidden, w_down_ref[inner, :])
            line_ref[n, p] = total.reshape(groups, cols, width).astype(BF16)
            for m in range(groups):
                r = m * SLAB + p * half + jnp.bitwise_xor(zi, k)
                copies.append(
                    pltpu.make_async_copy(line_ref.at[n, p, m], out_ref.at[r], sems.at[len(copies)])
                )
                copies[-1].start()
    for copy in copies:
        copy.wait()


def feed(places, sections, weights, image, partial):
    rows, cols, width = image.shape
    groups = rows // SLAB
    hidden = weights[2].shape[1]
    held = len(sections) + len(weights)
    count = len(places) * rows * cols // 4
    extra = [] if partial is None else [partial]
    return pl.pallas_call(
        functools.partial(feed_kernel, places),
        in_specs=[VMEM] * held + [ANY] * len(extra),
        out_specs=ANY,
        out_shape=jax.ShapeDtypeStruct(image.shape, BF16),
        scratch_shapes=[
            pltpu.VMEM((len(places), 2, groups, cols, width), BF16),
            pltpu.VMEM((len(places), 2, cols // SLAB, groups * SLAB, width), F32),
            pltpu.SemaphoreType.DMA((2 * len(places) * groups,)),
        ],
        input_output_aliases={held: 0} if extra else {},
        compiler_params=PARAMS,
        cost_estimate=pl.CostEstimate(
            flops=4 * count * width * hidden, bytes_accessed=2_000_000, transcendentals=count * hidden
        ),
        name="feed",
    )(*sections, *weights, *extra)


def local(
    image,
    bn_gain,
    bn_shift,
    w_expand,
    b_expand,
    w_depth,
    b_depth,
    w_project,
    b_project,
    attn_gain,
    attn_shift,
    w_qkv,
    w_out,
    rel_table,
    ffn_gain,
    ffn_shift,
    w_up,
    b_up,
    w_down,
    b_down,
):
    rows, cols, width = image.shape
    strips = lax.axis_size("strip")
    tiles = lax.axis_size("tile")
    col_groups = tiles // GRID
    assert strips == 2 and rows * strips == GRID * SLAB and cols == 4 * SLAB

    def row(v):
        return v.reshape(1, -1)

    def exchange(value, mask):
        pairs = []
        for g in range(GRID):
            for c in range(col_groups):
                for s in range(strips):
                    member = (g * strips + s) ^ mask
                    source = (g * col_groups + c) * strips + s
                    target = ((member // strips) * col_groups + c) * strips + member % strips
                    pairs.append((source, target))
        return lax.ppermute(value, ("tile", "strip"), pairs)

    beyond = lax.ppermute(border(image), "strip", [(0, 1), (1, 0)])
    to_even, to_odd = edges(image, beyond)
    even_pairs = [(i, i ^ 1) for i in range(tiles)]
    odd_pairs = [(i, i + 1) for i in range(1, tiles - 1, 2)]
    odd_pairs = odd_pairs + [(j, i) for i, j in odd_pairs]
    odd = lax.ppermute(to_odd, "tile", odd_pairs)
    even = lax.ppermute(to_even, "tile", even_pairs)

    vectors_in = (row(bn_gain), row(bn_shift), row(b_expand), row(b_depth), row(b_project), w_depth)
    expanded, vectors = expand(image, w_expand, vectors_in)
    taps, outer = rim(rows, even, odd, beyond, w_expand, vectors)
    attend_weights = (row(attn_gain), row(attn_shift), w_qkv, w_out, table(rel_table))
    feed_weights = (row(ffn_gain), row(ffn_shift), w_up, row(b_up), w_down, row(b_down))
    heads = rel_table.shape[0]

    def after(first, then):
        return lax.optimization_barrier((first, then))

    def to_peer(outgoing, key):
        return exchange(outgoing[key], 4 * key[0] + 2 * key[1])

    far_keys = ((3, 0), (2, 0), (3, 1), (2, 1))
    near_keys = ((1, 0), (0, 1), (1, 1))

    def paired(own, from_core, first):
        return {
            (first + k, x): jnp.stack([own[k, x], from_core[k, x]]) for k in range(own.shape[0]) for x in range(2)
        }

    def spread(own_f, to_core_f, own_n, to_core_n):
        outgoing = paired(own_f, exchange(to_core_f, 1), 2)
        arrived = {key: to_peer(outgoing, key) for key in far_keys}
        outgoing = paired(own_n, exchange(to_core_n, 1), 0)
        arrived[0, 0] = outgoing[0, 0]
        arrived.update({key: to_peer(outgoing, key) for key in near_keys})
        return [arrived[k, x] for k in range(4) for x in range(2)]

    held = spread(*conv(expanded, image, taps, outer, w_project, vectors))
    home = spread(*attend(held, heads, attend_weights))
    return feed((0, 1, 2, 3), home, feed_weights, image, None)


def solution(mesh):
    return jax.shard_map(
        local,
        mesh=mesh,
        in_specs=(P(("group", "strip"), "tile", None),) + (P(),) * 19,
        out_specs=P(("group", "strip"), "tile", None),
        check_vma=False,
    )
```
